512 devices in a mesh: pipe: 16 (over z), dp: 32 (over x, y, core).
Axes of the slice: x: 4, y: 4, z: 16, core: 2. Of those that a mesh axis runs over, the one named last changes fastest.
Arguments:
- hidden: bfloat16 [4096, 2048], P('dp', 'pipe'), may hold values from -6 to 6
- lengths: int32 [512, 4], P('dp'), may hold values from 1 to 3, as said below
- route: int32 [512, 2], P('dp'), may hold values from 0 to 31, as said below
- gain: float32 [32, 2048], P('pipe'), may hold values from 0.5 to 1.5
- key_weight: bfloat16 [32, 2048, 128], P('pipe'), may hold values from -0.125 to 0.125
- value_weight: bfloat16 [32, 2048, 128], P('pipe'), may hold values from -0.125 to 0.125
- cotangent: bfloat16 [4096, 2048], P('dp'), may hold values from -6 to 6
Outputs:
- input_grad: bfloat16 [4096, 2048], P('dp', 'pipe')
- key_grad: float32 [32, 2048, 128], P('pipe', 'dp')
- value_grad: float32 [32, 2048, 128], P('pipe', 'dp')
The draws below stay inside these ranges and needn't reach their ends.
Inputs may be any that keep to these rules, and one draw needn't show every extreme that they name: `lengths`: in every micro-batch the first 2 documents fill exactly the first 4 rows, and the others the rest. `route`: for each micro-batch index and each column, the destinations of the 32 groups are all different; and the 32 halves of one group go to 32 different groups.
All inputs are finite; a program needn't handle non-finite values.
Results may differ from the reference program's by a relative error of at most 0.035.
Values may be sent and summed in bfloat16 or wider, within the bound.
A program may use at most 64 MiB of HBM per device.

```python
import jax
import jax.numpy as jnp
from jax import lax

DH = 128
S = 8
DOCS = 4
MB = 16
F = 2048
GROUPS = 32
LAYERS = 32
N_PIPE = 16
N_DP = 32


def draw_lengths(key, part):
    key = jax.random.fold_in(key, 11)
    half_rows = S // 2
    per_half = DOCS // 2
    row_keys = jax.random.split(key, GROUPS * MB * 2)

    def one_half(row_key):
        shuffled = jax.random.permutation(row_key, half_rows - 1) + 1
        cuts = jnp.sort(shuffled[:per_half - 1]).astype(jnp.int32)
        bounds = jnp.concatenate([jnp.zeros((1,), jnp.int32), cuts, jnp.full((1,), half_rows, jnp.int32)])
        return bounds[1:] - bounds[:-1]
    halves = jax.vmap(one_half)(row_keys)
    forced = jnp.concatenate([jnp.ones((per_half - 1,), jnp.int32), jnp.full((1,), half_rows - per_half + 1, jnp.int32)])
    halves = halves.at[0].set(forced)
    return halves.reshape(GROUPS * MB, DOCS).astype(jnp.int32)


def draw_route(key, part):
    key = jax.random.fold_in(key, 12)
    first_key, second_key, third_key = jax.random.split(key, 3)
    row_shift = jax.random.permutation(first_key, GROUPS).astype(jnp.int32)
    column_shift = jax.random.permutation(second_key, GROUPS).astype(jnp.int32)
    relabel = jax.random.permutation(third_key, GROUPS).astype(jnp.int32)
    square = (row_shift[:, None] + column_shift[None, :]) % GROUPS
    return relabel[square].reshape(GROUPS * MB, 2).astype(jnp.int32)


def block_levels(key, extent, cuts, low, top_value):
    level, own = 1.0, jax.random.fold_in(key, 6)
    for dim, parts in cuts:
        heights = jnp.exp(jax.random.uniform(jax.random.fold_in(own, dim), (parts,), jnp.float32, low / len(cuts), top_value / len(cuts)))
        level = level * jnp.repeat(heights, extent[dim] // parts).reshape([-1 if axis == dim else 1 for axis in range(len(extent))])
    return level


def normal_values(stream_key, extent, spread, limit, shards=(), kind=jnp.bfloat16):
    drawn = jax.random.normal(stream_key, extent, jnp.float32) * spread
    if len(shards) > 0:
        drawn = block_levels(stream_key, extent, shards, -0.22, 0.18) * drawn
    return jnp.clip(drawn, min=-limit, max=limit).astype(kind)


def setup_inputs(seed: int = 0) -> dict:
    key_of = jax.random.split(jax.random.key(seed), 8)
    return {
        "hidden": normal_values(key_of[0], (GROUPS * MB * S, F), 1.0, 6.0, ((0, 32), (1, 16))),
        "lengths": draw_lengths(jax.random.fold_in(key_of[7], 71), 0),
        "route": draw_route(jax.random.fold_in(key_of[7], 71), 0),
        "gain": jnp.clip(1.0 + 0.1 * jax.random.normal(key_of[3], (LAYERS, F), jnp.float32), 0.5, 1.5),
        "key_weight": normal_values(key_of[4], (LAYERS, F, DH), F ** -0.5, 0.125, ((0, 16),)),
        "value_weight": normal_values(key_of[5], (LAYERS, F, DH), F ** -0.5, 0.125, ((0, 16),)),
        "cotangent": normal_values(key_of[6], (GROUPS * MB * S, F), 1.0, 6.0, ((0, 32),)),
    }


ROPE_BASE = 500000.0
EPSILON = 1e-05
NEGATIVE = -1e+30

def document_positions(lengths, row_count):
    doc_ends = jnp.cumsum(lengths, axis=-1).astype(jnp.int32)
    doc_starts = doc_ends - lengths
    row_numbers = jnp.arange(row_count, dtype=jnp.int32)
    document = lax.optimization_barrier(jnp.sum((row_numbers[None, :, None] >= doc_ends[:, None, :-1]).astype(jnp.int32), axis=-1, dtype=jnp.int32))
    picked = document[:, :, None] == jnp.arange(lengths.shape[1], dtype=jnp.int32)[None, None, :]
    opening = lax.optimization_barrier(jnp.sum(jnp.where(picked, doc_starts[:, None, :], 0), axis=-1, dtype=jnp.int32))
    return (document, row_numbers[None, :] - opening)

def rotary_tables(position, head_size):
    frequency = ROPE_BASE ** (-(jnp.arange(head_size // 2, dtype=jnp.float32) * 2.0 / head_size))
    angles = position.astype(jnp.float32)[..., None] * frequency
    return (jnp.cos(angles), jnp.sin(angles))

def rotate(vectors, cosine_table, sine_table):
    midpoint = vectors.shape[-1] // 2
    front_half = vectors[..., :midpoint]
    rear_half = vectors[..., midpoint:]
    return jnp.concatenate([front_half * cosine_table - rear_half * sine_table, rear_half * cosine_table + front_half * sine_table], axis=-1)

def normalize(hidden_in, gain_row):
    widened = hidden_in.astype(jnp.float32)
    return widened * lax.rsqrt(lax.optimization_barrier(jnp.mean(widened * widened, axis=-1, keepdims=True)) + EPSILON) * gain_row

def attend_layer(hidden_in, gain_row, key_proj, value_proj, key_zero, value_zero, document, position, cosine_table, sine_table):
    batch_count, row_count, feature_count = hidden_in.shape
    head_size = key_proj.shape[1]
    head_count = feature_count // head_size
    widened = hidden_in.astype(jnp.float32)
    normed = normalize(hidden_in, gain_row)
    packed = normed.astype(jnp.bfloat16)
    flattened = packed.reshape(batch_count * row_count, feature_count)
    key_pre = jnp.dot(flattened, key_proj, preferred_element_type=jnp.float32).reshape(batch_count, row_count, head_size) + key_zero
    value_pre = jnp.dot(flattened, value_proj, preferred_element_type=jnp.float32).reshape(batch_count, row_count, head_size) + value_zero
    queries = rotate(normed.reshape(batch_count, row_count, head_count, head_size), cosine_table[:, :, None, :], sine_table[:, :, None, :]).astype(jnp.bfloat16)
    key_vecs = rotate(key_pre, cosine_table, sine_table).astype(jnp.bfloat16)
    values = value_pre.astype(jnp.bfloat16)
    scores = jnp.einsum('bshd,btd->bhst', queries.astype(jnp.float32), key_vecs.astype(jnp.float32)) * head_size ** (-0.5)
    allowed = (document[:, :, None] == document[:, None, :]) & (position[:, None, :] <= position[:, :, None])
    scores = jnp.where(allowed[:, None, :, :], scores, NEGATIVE)
    ceiling = lax.stop_gradient(lax.optimization_barrier(jnp.max(scores, axis=-1, keepdims=True)))
    raised = jnp.exp(scores - ceiling)
    weights = (raised / lax.optimization_barrier(jnp.sum(raised, axis=-1, keepdims=True))).astype(jnp.bfloat16)
    mixture = jnp.einsum('bhst,btd->bshd', weights.astype(jnp.float32), values.astype(jnp.float32)).reshape(batch_count, row_count, feature_count)
    return widened + mixture

def reference(hidden, lengths, route, gain, key_weight, value_weight, cotangent):
    groups = N_DP
    sections = N_PIPE
    layers = 2 * sections
    half_rows = S // 2
    document, position = document_positions(lengths, S)
    document = document.reshape(groups, MB, S)
    position = position.reshape(groups, MB, S)
    source_of = jnp.argsort(route.reshape(groups, MB, 2), axis=0).astype(jnp.int32)
    batch_numbers = jnp.arange(MB, dtype=jnp.int32)[None, :]

    def arrange(source):
        leading = source[:, :, :half_rows][source_of[:, :, 0], batch_numbers]
        trailing = source[:, :, half_rows:][source_of[:, :, 1], batch_numbers]
        return jnp.concatenate([leading, trailing], axis=2)
    recv_document = arrange(document).reshape(groups * MB, S)
    recv_position = arrange(position).reshape(groups * MB, S)
    cosine_table, sine_table = rotary_tables(recv_position, DH)

    def slot_of(layer_index):
        return 2 * (layer_index % sections) + layer_index // sections

    def network(source, key_zeros, value_zeros):
        current = arrange(source.reshape(groups, MB, S, F)).reshape(groups * MB, S, F).astype(jnp.float32)
        inputs = []
        for layer_index in range(layers):
            weight_slot = slot_of(layer_index)
            inputs.append(current)
            current = attend_layer(current, gain[weight_slot], key_weight[weight_slot], value_weight[weight_slot], key_zeros[layer_index], value_zeros[layer_index], recv_document, recv_position, cosine_table, sine_table)
        return (current, inputs)
    zero_terms = jnp.zeros((layers, groups * MB, S, DH), jnp.float32)
    final_rows, pullback, inputs = jax.vjp(network, hidden, zero_terms, zero_terms, has_aux=True)
    source_grad, key_pre_grad, value_pre_grad = pullback(cotangent.astype(jnp.float32).reshape(groups * MB, S, F))
    key_rows = [None] * layers
    value_rows = [None] * layers
    for layer_index in range(layers):
        weight_slot = slot_of(layer_index)
        packed = normalize(inputs[layer_index], gain[weight_slot]).astype(jnp.bfloat16).reshape(groups * MB * S, F)
        key_rows[weight_slot] = jnp.dot(packed.T, key_pre_grad[layer_index].astype(jnp.bfloat16).reshape(groups * MB * S, DH), preferred_element_type=jnp.float32)
        value_rows[weight_slot] = jnp.dot(packed.T, value_pre_grad[layer_index].astype(jnp.bfloat16).reshape(groups * MB * S, DH), preferred_element_type=jnp.float32)
    return (source_grad.astype(jnp.bfloat16).reshape(groups * MB * S, F), jnp.stack(key_rows), jnp.stack(value_rows))
```

```python
import jax
import jax.numpy as jnp
from jax import lax
from jax.experimental import pallas as pl
from jax.experimental.pallas import tpu as pltpu
from jax.sharding import PartitionSpec as P

ROPE_BASE = 500000.0
EPSILON = 1e-05
NEGATIVE = -1e30
HEADS = 16
ROWS = 8
HEAD = 128
F32 = jnp.float32
BF16 = jnp.bfloat16


def document_positions(lengths, row_count):
    doc_ends = jnp.cumsum(lengths, axis=-1)
    doc_starts = doc_ends - lengths
    row_numbers = jnp.arange(row_count, dtype=jnp.int32)
    document = jnp.sum(
        (row_numbers[None, :, None] >= doc_ends[:, None, :-1]).astype(jnp.int32),
        axis=-1,
        dtype=jnp.int32,
    )
    picked = document[:, :, None] == jnp.arange(lengths.shape[1], dtype=jnp.int32)[None, None, :]
    opening = jnp.sum(jnp.where(picked, doc_starts[:, None, :], 0), axis=-1, dtype=jnp.int32)
    return (document, row_numbers[None, :] - opening)


def dot(a, b, over_a, over_b):
    return lax.dot_general(
        a, b, (((over_a,), (over_b,)), ((), ())), preferred_element_type=F32
    )


def swap_halves(flat):
    return pltpu.roll(flat, HEAD // 2, 1)


def turn(flat, cosine, sine):
    return flat * cosine + swap_halves(flat) * sine


def unturn(flat, cosine, sine):
    return flat * cosine - swap_halves(flat) * sine


def side_by_side(flat):
    return jnp.concatenate([flat[ROWS * h:ROWS * (h + 1)] for h in range(HEADS)], axis=1)


def stacked(wide):
    return jnp.concatenate([wide[:, HEAD * h:HEAD * (h + 1)] for h in range(HEADS)], axis=0)


def row_mean(flat):
    total = jnp.sum(flat.reshape(HEADS, ROWS, HEAD), axis=0)
    return jnp.sum(total, axis=-1, keepdims=True) * (1.0 / (HEADS * HEAD))


def over_heads(rows):
    return jnp.broadcast_to(rows[None], (HEADS, ROWS, rows.shape[-1])).reshape(
        HEADS * ROWS, rows.shape[-1]
    )


def gain_rows(gain):
    return jnp.broadcast_to(gain[:, None, :], (HEADS, ROWS, HEAD)).reshape(HEADS * ROWS, HEAD)


def layers_kernel(
    start_ref, last_ref, cos_ref, sin_ref, bias_ref, gain_ref, weight_ref,
    packed_ref, pair_ref, grad_ref,
    current, saved, saved_queries, saved_keys, saved_weights, saved_scale,
):
    step = pl.program_id(0)
    layers = gain_ref.shape[0]
    weight = weight_ref[...].reshape(HEADS * HEAD, 2 * HEAD)
    cosine, sine = cos_ref[...], sin_ref[...]
    cosine_all, sine_all = over_heads(cosine), over_heads(sine)

    @pl.when(step == 0)
    def _():
        current[...] = start_ref[...].astype(F32)

    @pl.when(step < layers)
    def _():
        x = current[...]
        saved[step] = x
        scale = lax.rsqrt(row_mean(x * x) + EPSILON)
        saved_scale[step] = scale
        normed = x * over_heads(scale) * gain_rows(gain_ref[step])
        packed = side_by_side(normed).astype(BF16)
        packed_ref[step] = packed
        pre = dot(packed, weight, 1, 0)
        keys = turn(pre[:, :HEAD], cosine, sine).astype(BF16)
        values = pre[:, HEAD:].astype(BF16)
        queries = turn(normed, cosine_all, sine_all).astype(BF16)
        scores = dot(keys, queries, 1, 1) * HEAD ** (-0.5) + bias_ref[...]
        raised = jnp.exp(scores - jnp.max(scores, axis=0, keepdims=True))
        weights = raised / jnp.sum(raised, axis=0, keepdims=True)
        saved_queries[step] = queries
        saved_keys[step, 0] = keys
        saved_keys[step, 1] = values
        saved_weights[step] = weights
        current[...] = x + dot(weights.astype(BF16), values, 0, 0)

    @pl.when(step == layers)
    def _():
        current[...] = last_ref[...].astype(F32)

    @pl.when(step >= layers)
    def _():
        layer = 2 * layers - 1 - step
        upstream = current[...]
        rounded = upstream.astype(BF16)
        keys = saved_keys[layer, 0]
        values = saved_keys[layer, 1]
        weights = saved_weights[layer]
        d_weights = dot(values, rounded, 1, 1).astype(BF16).astype(F32)
        d_values = dot(weights.astype(BF16), rounded, 1, 0).astype(BF16).astype(F32)
        inner = jnp.sum(d_weights * weights, axis=0, keepdims=True)
        d_scores = (weights * (d_weights - inner) * HEAD ** (-0.5)).astype(BF16)
        d_queries = dot(d_scores, keys, 0, 0).astype(BF16).astype(F32)
        d_keys = dot(d_scores, saved_queries[layer], 1, 0).astype(BF16).astype(F32)
        d_key_pre = unturn(d_keys, cosine, sine)
        pair = jnp.concatenate([d_key_pre, d_values], axis=1).astype(BF16)
        pair_ref[layer] = pair
        d_packed = stacked(dot(pair, weight, 1, 1))
        d_normed = unturn(d_queries, cosine_all, sine_all) + d_packed
        x = saved[layer]
        scale = saved_scale[layer]
        scaled = d_normed * gain_rows(gain_ref[layer])
        pull = row_mean(scaled * x) * scale * scale * scale
        current[...] = upstream + scaled * over_heads(scale) - x * over_heads(pull)

    @pl.when(step == 2 * layers - 1)
    def _():
        grad_ref[...] = current[...].astype(BF16)


def run_layers(start, last, cosine, sine, bias, gain, weight, sections, features, interpret=False):
    layers = gain.shape[0]
    parts = weight.shape[0]

    def block_of(step):
        layer = jnp.where(step < layers, step, 2 * layers - 1 - step)
        return (0, layer % sections, layer // sections, 0, 0)

    whole = pl.BlockSpec(memory_space=pltpu.VMEM)
    tile = HEADS * ROWS
    return pl.pallas_call(
        layers_kernel,
        grid=(2 * layers,),
        out_shape=(
            jax.ShapeDtypeStruct((layers, ROWS, HEADS * HEAD), BF16),
            jax.ShapeDtypeStruct((layers, ROWS, 2 * HEAD), BF16),
            jax.ShapeDtypeStruct((tile, HEAD), BF16),
        ),
        in_specs=[whole] * 6
        + [pl.BlockSpec((parts, 1, 1, features // parts, 2 * HEAD), block_of)],
        out_specs=(whole, whole, whole),
        scratch_shapes=[
            pltpu.VMEM((tile, HEAD), F32),
            pltpu.VMEM((layers, tile, HEAD), F32),
            pltpu.VMEM((layers, tile, HEAD), BF16),
            pltpu.VMEM((layers, 2, ROWS, HEAD), BF16),
            pltpu.VMEM((layers, ROWS, tile), F32),
            pltpu.VMEM((layers, ROWS, 1), F32),
        ],
        compiler_params=pltpu.CompilerParams(vmem_limit_bytes=40 * 2**20),
        interpret=interpret,
    )(start, last, cosine, sine, bias, gain, weight)


def attention_tables(document, position):
    half = HEAD // 2
    frequency = ROPE_BASE ** (-(jnp.arange(half, dtype=F32) * 2.0 / HEAD))
    angles = position.astype(F32)[:, None] * frequency
    cosine, sine = jnp.cos(angles), jnp.sin(angles)
    allowed = (document[:, None] == document[None, :]) & (position[:, None] <= position[None, :])
    bias = jnp.where(allowed, 0.0, NEGATIVE).astype(F32)
    return (
        jnp.concatenate([cosine, cosine], axis=-1),
        jnp.concatenate([-sine, sine], axis=-1),
        jnp.tile(bias, (1, HEADS)),
    )


def body(hidden, lengths, route, gain, key_weight, value_weight, cotangent):
    groups = lax.axis_size("dp")
    sections = lax.axis_size("pipe")
    group = lax.axis_index("dp")
    section = lax.axis_index("pipe")
    micro_count = lengths.shape[0]
    source_rows, columns = hidden.shape
    half_rows = ROWS // 2
    half_count = 2 * micro_count
    features = gain.shape[1]
    part = features // groups

    both = jnp.concatenate([key_weight, value_weight], axis=-1)
    share = lax.dynamic_slice_in_dim(both, group * part, part, 1)
    column = lax.all_gather(share, "pipe", axis=0, tiled=False)
    weight = lax.all_gather(column, "dp", axis=0, tiled=False)
    gains = lax.all_gather(gain, "pipe", axis=0, tiled=False)
    gains = jnp.swapaxes(gains, 0, 1).reshape(2 * sections, HEADS, HEAD)

    document, position = document_positions(lengths, ROWS)
    tags = (document * ROWS + position).reshape(half_count, half_rows)
    slots = jnp.arange(half_count, dtype=jnp.int32)
    route_flat = route.reshape(half_count)
    label = jnp.concatenate([tags, slots[:, None]], axis=1)
    label = jnp.pad(label, ((0, 0), (0, columns - half_rows - 1))).astype(BF16)
    packet = jnp.concatenate([hidden.reshape(half_count, half_rows * columns), label], axis=1)
    chosen = (route_flat[None, :] == jnp.arange(groups, dtype=jnp.int32)[:, None]).astype(BF16)
    outgoing = jnp.dot(chosen, packet, preferred_element_type=F32).astype(BF16)
    arrived = lax.all_to_all(outgoing, "dp", split_axis=0, concat_axis=0, tiled=True)
    arrived_label = arrived[:, half_rows * columns:]
    arrived_slots = arrived_label[:, half_rows].astype(jnp.int32)
    placing = (arrived_slots[None, :] == slots[:, None]).astype(BF16)
    received = jnp.dot(placing, arrived, preferred_element_type=F32).astype(BF16)
    row_tags = received[:, half_rows * columns:half_rows * columns + half_rows]
    row_tags = row_tags.astype(jnp.int32).reshape(micro_count, ROWS)
    own_tags = lax.dynamic_index_in_dim(row_tags, section, 0, keepdims=False)
    rows = received[:, :half_rows * columns].reshape(micro_count, ROWS, columns)
    start = lax.all_to_all(rows, "pipe", split_axis=0, concat_axis=0, tiled=True)
    start = start.reshape(HEADS * ROWS, HEAD)
    cosine, sine, bias = attention_tables(own_tags // ROWS, own_tags % ROWS)
    last = lax.dynamic_slice_in_dim(cotangent, section * ROWS, ROWS, 0)
    last = jnp.swapaxes(last.reshape(ROWS, HEADS, HEAD), 0, 1).reshape(HEADS * ROWS, HEAD)

    packed, pairs, grads = run_layers(
        start, last, cosine, sine, bias, gains, weight, sections, features
    )

    mine = lax.all_to_all(
        grads.reshape(sections, ROWS, columns), "pipe", split_axis=0, concat_axis=0, tiled=True
    )
    mine = mine.reshape(half_count, half_rows * columns)
    returning = jnp.dot(placing.T, mine, preferred_element_type=F32).astype(BF16)
    returned = lax.all_to_all(returning, "dp", split_axis=0, concat_axis=0, tiled=True)
    source_grad = jnp.dot(chosen.T, returned, preferred_element_type=F32).astype(BF16)

    layer_packed = lax.all_to_all(
        packed.reshape(2, sections, ROWS, features), "pipe", split_axis=1, concat_axis=1, tiled=True
    )
    layer_pairs = lax.all_to_all(
        pairs.reshape(2, sections, ROWS, 2 * HEAD), "pipe", split_axis=1, concat_axis=1, tiled=True
    )
    terms = jnp.einsum("vmsw,vmsc->wvc", layer_packed, layer_pairs, preferred_element_type=F32)
    summed = lax.psum_scatter(
        terms.astype(BF16).reshape(features, 4 * HEAD), "dp", scatter_dimension=0, tiled=True
    )
    summed = summed.astype(F32).reshape(part, 2, 2, HEAD)
    key_out = jnp.transpose(summed[:, :, 0, :], (1, 0, 2))
    value_out = jnp.transpose(summed[:, :, 1, :], (1, 0, 2))
    return (source_grad.reshape(source_rows, columns), key_out, value_out)


def solution(mesh):
    placed = (
        P("dp", "pipe"),
        P("dp", None),
        P("dp", None),
        P("pipe", None),
        P("pipe", None, None),
        P("pipe", None, None),
        P("dp", None),
    )
    return jax.shard_map(
        body,
        mesh=mesh,
        in_specs=placed,
        out_specs=(P("dp", "pipe"), P("pipe", "dp", None), P("pipe", "dp", None)),
        check_vma=False,
    )
```

```python
import jax
import jax.numpy as jnp
from jax import lax
from jax.experimental import pallas as pl
from jax.experimental.pallas import tpu as pltpu
from jax.sharding import PartitionSpec as P

ROPE_BASE = 500000.0
EPSILON = 1e-05
NEGATIVE = -1e30
HEADS = 16
ROWS = 8
HEAD = 128
SECTIONS = 16
GROUPS = 32
LAYERS = 32
SIDE = 4
PART = 64
TILE = HEADS * ROWS
FEATURES = HEADS * HEAD
F32 = jnp.float32
BF16 = jnp.bfloat16
MESH = pl.DeviceIdType.MESH


def document_positions(lengths, row_count):
    doc_ends = jnp.cumsum(lengths, axis=-1)
    doc_starts = doc_ends - lengths
    row_numbers = jnp.arange(row_count, dtype=jnp.int32)
    document = jnp.sum(
        (row_numbers[None, :, None] >= doc_ends[:, None, :-1]).astype(jnp.int32),
        axis=-1,
        dtype=jnp.int32,
    )
    picked = document[:, :, None] == jnp.arange(lengths.shape[1], dtype=jnp.int32)[None, None, :]
    opening = jnp.sum(jnp.where(picked, doc_starts[:, None, :], 0), axis=-1, dtype=jnp.int32)
    return (document, row_numbers[None, :] - opening)


def dot(a, b, over_a, over_b):
    return lax.dot_general(
        a, b, (((over_a,), (over_b,)), ((), ())), preferred_element_type=F32
    )


def swap_halves(flat):
    return pltpu.roll(flat, HEAD // 2, 1)


def turn(flat, cosine, sine):
    return flat * cosine + swap_halves(flat) * sine


def unturn(flat, cosine, sine):
    return flat * cosine - swap_halves(flat) * sine


def side_by_side(flat):
    return jnp.concatenate([flat[ROWS * h:ROWS * (h + 1)] for h in range(HEADS)], axis=1)


def stacked(wide):
    return jnp.concatenate([wide[:, HEAD * h:HEAD * (h + 1)] for h in range(HEADS)], axis=0)


def row_mean(flat):
    total = jnp.sum(flat.reshape(HEADS, ROWS, HEAD), axis=0)
    return jnp.sum(total, axis=-1, keepdims=True) * (1.0 / (HEADS * HEAD))


def over_heads(rows):
    return jnp.broadcast_to(rows[None], (HEADS, ROWS, rows.shape[-1])).reshape(
        HEADS * ROWS, rows.shape[-1]
    )


def gain_rows(gain):
    return jnp.broadcast_to(gain[:, None, :], (HEADS, ROWS, HEAD)).reshape(HEADS * ROWS, HEAD)


def whole_kernel(
    source_ref, lane_route_ref, last_ref, cos_ref, sin_ref, gain_ref, key_ref, value_ref,
    grad_ref, key_out_ref, value_out_ref,
    weight, gains, current, saved, saved_queries, saved_keys, saved_weights, saved_scale, bias, turns,
    packed_all, packed_in, pairs_all, pairs_in, terms, twin_in, chip_terms, chip_in,
    sorting, placing, half_out, half_in, rows_out, rows_in, back_out, back_in, home_out, home_in,
    own_sem, zw_recv, zw_right, zw_left, zg_recv, zg_right, zg_left,
    ring_send, ring_recv, packed_send, packed_recv, pair_send, pair_recv,
    half_send, half_recv, rows_send, rows_recv, back_send, back_recv, home_send, home_recv,
    twin_send, twin_recv, chip_send, chip_recv,
):
    z = lax.axis_index("pipe")
    d = lax.axis_index("dp")
    core = d % 2
    chip = d // 2
    px, py = chip // SIDE, chip % SIDE
    twin = chip * 2 + 1 - core
    z_next, z_before = (z + 1) % SECTIONS, (z + SECTIONS - 1) % SECTIONS

    def remote(src, dst, send, recv, to_z, to_d):
        return pltpu.make_async_remote_copy(
            src_ref=src, dst_ref=dst, send_sem=send, recv_sem=recv,
            device_id={"pipe": to_z, "dp": to_d}, device_id_type=MESH,
        )

    def await_recv(ref, sem):
        remote(ref, ref, sem, sem, z, twin).wait_recv()

    def await_send(ref, sem):
        remote(ref, ref, sem, sem, z, twin).wait_send()

    def loop(low, high, run):
        lax.fori_loop(low, high, lambda i, c: (run(i), c)[1], 0)

    owned = []
    for v in range(2):
        layer = v * SECTIONS + z
        rows = pl.ds(pl.multiple_of(d * PART, PART), PART)
        own = weight.at[layer, px, py, core]
        owned.append(pltpu.make_async_copy(
            key_ref.at[v, rows, :], own.at[:, pl.ds(0, HEAD)], own_sem.at[v, 0]))
        owned.append(pltpu.make_async_copy(
            value_ref.at[v, rows, :], own.at[:, pl.ds(HEAD, HEAD)], own_sem.at[v, 1]))
    for copy in owned:
        copy.start()
    for v in range(2):
        gains[v * SECTIONS + z] = gain_ref[v]

    row = lax.broadcasted_iota(jnp.int32, (2 * TILE, 2 * TILE), 0)
    col = lax.broadcasted_iota(jnp.int32, (2 * TILE, 2 * TILE), 1)
    kind_row = (col // TILE) * (ROWS // 2) + col % (ROWS // 2)
    sort = jnp.where((lane_route_ref[...] == row // ROWS) & (row % ROWS == kind_row), 1.0, 0.0)
    sort = sort.astype(BF16)
    sorting[...] = sort[:, :TILE]
    half_out[...] = dot(sort, source_ref[...], 1, 0).reshape(GROUPS, ROWS, HEAD)
    half_in[d] = half_out[d]

    barrier = pltpu.get_barrier_semaphore()

    def greet_plane(k):
        pl.semaphore_signal(
            barrier, inc=1, device_id={"pipe": z, "dp": (d + k) % GROUPS}, device_id_type=MESH)

    def greet_line(k):
        pl.semaphore_signal(
            barrier, inc=1, device_id={"pipe": (z + k) % SECTIONS, "dp": d}, device_id_type=MESH)

    loop(1, GROUPS, greet_plane)
    loop(1, SECTIONS, greet_line)
    pl.semaphore_wait(barrier, GROUPS + SECTIONS - 2)

    def send_half(k):
        to = (d + k) % GROUPS
        remote(half_out.at[to], half_in.at[d], half_send.at[to], half_recv.at[d], z, to).start()

    for copy in owned:
        copy.wait()

    def line_step(v, s):
        from_left = v * SECTIONS + (z + SECTIONS - s) % SECTIONS
        from_right = v * SECTIONS + (z + s) % SECTIONS

        @pl.when(s >= 1)
        def _():
            await_recv(weight.at[from_left, px, py, core], zw_recv.at[from_left])
            await_recv(gains.at[from_left], zg_recv.at[from_left])

        @pl.when(s <= 7)
        def _():
            own = weight.at[from_left, px, py, core]
            remote(own, own, zw_right.at[v, s], zw_recv.at[from_left], z_next, d).start()
            line = gains.at[from_left]
            remote(line, line, zg_right.at[v, s], zg_recv.at[from_left], z_next, d).start()

        @pl.when((s >= 1) & (s <= 7))
        def _():
            await_recv(weight.at[from_right, px, py, core], zw_recv.at[from_right])
            await_recv(gains.at[from_right], zg_recv.at[from_right])

        @pl.when(s <= 6)
        def _():
            own = weight.at[from_right, px, py, core]
            remote(own, own, zw_left.at[v, s], zw_recv.at[from_right], z_before, d).start()
            line = gains.at[from_right]
            remote(line, line, zg_left.at[v, s], zg_recv.at[from_right], z_before, d).start()

    line_step(0, 0)
    loop(1, GROUPS, send_half)
    loop(1, 4, lambda s: line_step(0, s))

    def await_half(k):
        at = (d + k) % GROUPS
        await_recv(half_in.at[at], half_recv.at[at])

    loop(1, GROUPS, await_half)
    arrived = half_in[...]
    slot = jnp.broadcast_to(arrived[:, 4:5, HEAD // 2:HEAD // 2 + 1], (GROUPS, ROWS, 1))
    slot = slot.reshape(2 * TILE, 1)
    arrived = arrived.reshape(2 * TILE, HEAD).astype(BF16)
    row = lax.broadcasted_iota(jnp.int32, (2 * TILE, TILE), 0) % ROWS
    col = lax.broadcasted_iota(jnp.int32, (2 * TILE, TILE), 1)
    same = slot == (col // (ROWS // 2)).astype(F32)
    place = jnp.where(same & (row == col % (ROWS // 2)), 1.0, 0.0).astype(BF16)
    place_tags = jnp.where(same & (row == col % (ROWS // 2) + ROWS // 2), 1.0, 0.0).astype(BF16)
    placing[...] = place
    rows_out[...] = dot(place, arrived, 0, 0).reshape(SECTIONS, ROWS, HEAD)
    home_out[pl.ds(0, SECTIONS)] = dot(place_tags, arrived, 0, 0).reshape(SECTIONS, ROWS, HEAD)
    rows_in[z] = rows_out[z]

    def send_rows(k):
        to = (z + k) % SECTIONS
        remote(rows_out.at[to], rows_in.at[z], rows_send.at[to], rows_recv.at[z], to, d).start()

    loop(1, SECTIONS, send_rows)

    tags = home_out[z]
    document = jnp.broadcast_to(tags[:, 0:1], (ROWS, TILE))
    position = jnp.broadcast_to(tags[:, HEAD // 4:HEAD // 4 + 1], (ROWS, TILE))
    lane = lax.broadcasted_iota(jnp.int32, (ROWS, TILE), 1) % ROWS
    mine = lane == lax.broadcasted_iota(jnp.int32, (ROWS, TILE), 0)
    query_document = jnp.sum(jnp.where(mine, document, 0.0), axis=0, keepdims=True)
    query_position = jnp.sum(jnp.where(mine, position, 0.0), axis=0, keepdims=True)
    allowed = (document == query_document) & (position <= query_position)
    bias[...] = jnp.where(allowed, 0.0, NEGATIVE)
    cosine = jnp.zeros((ROWS, HEAD), F32)
    sine = jnp.zeros((ROWS, HEAD), F32)
    for p in range(ROWS):
        cosine = jnp.where(position == float(p), cos_ref[p:p + 1, :], cosine)
        sine = jnp.where(position == float(p), sin_ref[p:p + 1, :], sine)
    turns[0] = cosine
    turns[1] = sine

    loop(4, 9, lambda s: line_step(0, s))

    def await_rows(k):
        at = (z + k) % SECTIONS
        await_recv(rows_in.at[at], rows_recv.at[at])

    loop(1, SECTIONS, await_rows)
    current[...] = rows_in[...].reshape(TILE, HEAD)

    def forward(layer):
        cosine, sine = turns[0], turns[1]
        cosine_all, sine_all = over_heads(cosine), over_heads(sine)
        x = current[...]
        saved[layer] = x
        scale = lax.rsqrt(row_mean(x * x) + EPSILON)
        saved_scale[layer] = scale
        normed = x * over_heads(scale) * gain_rows(gains[layer])
        wide = side_by_side(normed)
        pre = dot(wide.astype(BF16), weight[layer].reshape(FEATURES, 2 * HEAD), 1, 0)
        packed = jnp.concatenate(
            [wide[:, :FEATURES // 2], wide[:, FEATURES // 2:]], axis=0).astype(BF16)
        packed_all[layer] = packed
        owner, v = layer % SECTIONS, layer // SECTIONS

        @pl.when(owner != z)
        def _():
            remote(packed_all.at[layer], packed_in.at[v, z],
                   packed_send.at[layer], packed_recv.at[v, z], owner, d).start()

        @pl.when(owner == z)
        def _():
            packed_in[v, z] = packed

        keys = turn(pre[:, :HEAD], cosine, sine).astype(BF16)
        values = pre[:, HEAD:].astype(BF16)
        queries = turn(normed, cosine_all, sine_all).astype(BF16)
        scores = dot(keys, queries, 1, 1) * HEAD ** (-0.5) + bias[...]
        raised = jnp.exp(scores - jnp.max(scores, axis=0, keepdims=True))
        weights = raised / jnp.sum(raised, axis=0, keepdims=True)
        saved_queries[layer] = queries
        saved_keys[layer, 0] = keys
        saved_keys[layer, 1] = values
        saved_weights[layer] = weights
        current[...] = x + dot(weights.astype(BF16), values, 0, 0)

    def plane(layer, e, at_first, at_second, rows):
        if e == 0:
            first = px if at_first is None else at_first
            second = py if at_second is None else at_second
            if at_first is all:
                return weight.at[layer, :, second, core, rows, :]
            return weight.at[layer, first, second, core, rows, :]
        first = py if at_first is None else at_first
        second = px if at_second is None else at_second
        if at_first is all:
            return weight.at[layer, second, :, core, rows, :]
        return weight.at[layer, second, first, core, rows, :]

    def device_of(e, along_first, along_second):
        dx, dy = (along_first, along_second) if e == 0 else (along_second, along_first)
        return (((px + dx) % SIDE) * SIDE + (py + dy) % SIDE) * 2 + core

    every, low, high = pl.ds(0, PART), pl.ds(0, PART // 2), pl.ds(PART // 2, PART // 2)

    def around(e, which, by):
        base = (px if which == 0 else py) if e == 0 else (py if which == 0 else px)
        return (base + by) % SIDE

    def stage_one(layer, e):
        own = plane(layer, e, None, None, every)
        remote(own, own, ring_send.at[layer, 0], ring_recv.at[layer, 0], z, device_of(e, 1, 0)).start()
        remote(own, own, ring_send.at[layer, 0], ring_recv.at[layer, 1], z, device_of(e, 3, 0)).start()

    def stage_two(layer, e):
        left, right = around(e, 0, 3), around(e, 0, 1)
        await_recv(plane(layer, e, left, None, every), ring_recv.at[layer, 0])
        part = plane(layer, e, left, None, low)
        remote(part, part, ring_send.at[layer, 1], ring_recv.at[layer, 2], z, device_of(e, 1, 0)).start()
        await_recv(plane(layer, e, right, None, every), ring_recv.at[layer, 1])
        part = plane(layer, e, right, None, high)
        remote(part, part, ring_send.at[layer, 1], ring_recv.at[layer, 3], z, device_of(e, 3, 0)).start()

    def stage_three(layer, e):
        far = around(e, 0, 2)
        await_recv(plane(layer, e, far, None, low), ring_recv.at[layer, 2])
        await_recv(plane(layer, e, far, None, high), ring_recv.at[layer, 3])
        line = plane(layer, e, all, None, every)
        remote(line, line, ring_send.at[layer, 2], ring_recv.at[layer, 4], z, device_of(e, 0, 1)).start()
        remote(line, line, ring_send.at[layer, 2], ring_recv.at[layer, 5], z, device_of(e, 0, 3)).start()

    def stage_four(layer, e):
        left, right = around(e, 1, 3), around(e, 1, 1)
        await_recv(plane(layer, e, all, left, every), ring_recv.at[layer, 4])
        part = plane(layer, e, all, left, low)
        remote(part, part, ring_send.at[layer, 3], ring_recv.at[layer, 6], z, device_of(e, 0, 1)).start()
        await_recv(plane(layer, e, all, right, every), ring_recv.at[layer, 5])
        part = plane(layer, e, all, right, high)
        remote(part, part, ring_send.at[layer, 3], ring_recv.at[layer, 7], z, device_of(e, 0, 3)).start()

    def stage_five(layer, e):
        far = around(e, 1, 2)
        await_recv(plane(layer, e, all, far, low), ring_recv.at[layer, 6])
        await_recv(plane(layer, e, all, far, high), ring_recv.at[layer, 7])
        half = weight.at[layer, :, :, core]
        remote(half, half, ring_send.at[layer, 4], ring_recv.at[layer, 8], z, twin).start()

    def stage_six(layer, e):
        await_recv(weight.at[layer, :, :, 1 - core], ring_recv.at[layer, 8])
        forward(layer)

    stages = ((4, stage_five), (3, stage_four), (2, stage_three), (1, stage_two), (0, stage_one),
              (5, stage_six))
    pairs = LAYERS // 2

    def turn_of(t):
        @pl.when(t <= 8)
        def _():
            line_step(1, t)

        for late, stage in stages:
            @pl.when((t >= late) & (t < late + pairs))
            def _():
                for e in range(2):
                    stage(2 * (t - late) + e, e)

    loop(0, pairs + 5, turn_of)

    current[...] = last_ref[...]

    def backward(step):
        layer = LAYERS - 1 - step
        cosine, sine = turns[0], turns[1]
        cosine_all, sine_all = over_heads(cosine), over_heads(sine)
        upstream = current[...]
        rounded = upstream.astype(BF16)
        keys = saved_keys[layer, 0]
        values = saved_keys[layer, 1]
        weights = saved_weights[layer]
        d_weights = dot(values, rounded, 1, 1).astype(BF16).astype(F32)
        d_values = dot(weights.astype(BF16), rounded, 1, 0).astype(BF16).astype(F32)
        inner = jnp.sum(d_weights * weights, axis=0, keepdims=True)
        d_scores = (weights * (d_weights - inner) * HEAD ** (-0.5)).astype(BF16)
        d_queries = dot(d_scores, keys, 0, 0).astype(BF16).astype(F32)
        d_keys = dot(d_scores, saved_queries[layer], 1, 0).astype(BF16).astype(F32)
        d_key_pre = unturn(d_keys, cosine, sine)
        pair = jnp.concatenate([d_key_pre, d_values], axis=1)
        pairs_all[layer] = pair
        owner, v = layer % SECTIONS, layer // SECTIONS

        @pl.when(owner != z)
        def _():
            remote(pairs_all.at[layer], pairs_in.at[v, z],
                   pair_send.at[layer], pair_recv.at[v, z], owner, d).start()

        @pl.when(owner == z)
        def _():
            pairs_in[v, z] = pair

        d_packed = stacked(
            dot(pair.astype(BF16), weight[layer].reshape(FEATURES, 2 * HEAD), 1, 1))
        d_normed = unturn(d_queries, cosine_all, sine_all) + d_packed
        x = saved[layer]
        scale = saved_scale[layer]
        scaled = d_normed * gain_rows(gains[layer])
        pull = row_mean(scaled * x) * scale * scale * scale
        current[...] = upstream + scaled * over_heads(scale) - x * over_heads(pull)

    loop(0, LAYERS, backward)

    back_out[...] = current[...].astype(BF16).astype(F32).reshape(SECTIONS, ROWS, HEAD)
    back_in[z] = back_out[z]

    def send_back(k):
        to = (z + k) % SECTIONS
        remote(back_out.at[to], back_in.at[z], back_send.at[to], back_recv.at[z], to, d).start()

    loop(1, SECTIONS, send_back)

    for v in range(2):
        def await_rows_of(k):
            at = (z + k) % SECTIONS
            await_recv(packed_in.at[v, at], packed_recv.at[v, at])
            await_recv(pairs_in.at[v, at], pair_recv.at[v, at])

        loop(1, SECTIONS, await_rows_of)
        pair = pairs_in[v]
        nothing = jnp.zeros_like(pair)
        upper = jnp.concatenate([pair, nothing], axis=1).reshape(2 * TILE, 2 * HEAD)
        lower = jnp.concatenate([nothing, pair], axis=1).reshape(2 * TILE, 2 * HEAD)
        both = jnp.concatenate([upper, lower], axis=1).astype(BF16)
        product = dot(packed_in[v].reshape(2 * TILE, FEATURES // 2), both, 0, 0).astype(BF16)
        for g in range(GROUPS):
            rows = product[PART * (g % 16):PART * (g % 16 + 1)]
            terms[g // 2, g % 2, v] = rows[:, 2 * HEAD * (g // 16):2 * HEAD * (g // 16 + 1)]

    across = remote(terms.at[:, 1 - core], twin_in, twin_send, twin_recv, z, twin)
    across.start()

    def await_back(k):
        at = (z + k) % SECTIONS
        await_recv(back_in.at[at], back_recv.at[at])

    loop(1, SECTIONS, await_back)
    mine = back_in[...].reshape(TILE, HEAD).astype(BF16)
    home_out[...] = dot(placing[...], mine, 1, 0).reshape(GROUPS, ROWS, HEAD)
    home_in[d] = home_out[d]

    def send_home(k):
        to = (d + k) % GROUPS
        remote(home_out.at[to], home_in.at[d], home_send.at[to], home_recv.at[d], z, to).start()

    loop(1, GROUPS, send_home)

    across.wait()
    chip_terms[...] = (terms[:, core].astype(F32) + twin_in[...].astype(F32)).astype(BF16)

    def send_chip(k):
        to = (chip + k) % (GROUPS // 2)
        remote(chip_terms.at[to], chip_in.at[chip], chip_send.at[to], chip_recv.at[chip],
               z, 2 * to + core).start()

    loop(1, GROUPS // 2, send_chip)
    chip_in[chip] = chip_terms[chip]

    def await_home(k):
        at = (d + k) % GROUPS
        await_recv(home_in.at[at], home_recv.at[at])

    loop(1, GROUPS, await_home)
    arrived = home_in[...].reshape(2 * TILE, HEAD).astype(BF16)
    grad_ref[...] = dot(sorting[...], arrived, 0, 0).astype(BF16)

    def sent_layer(layer):
        await_send(weight.at[layer, pl.ds(0, 2), 0, 0], ring_send.at[layer, 0])
        await_send(weight.at[layer, 0, 0, 0], ring_send.at[layer, 1])
        await_send(weight.at[layer, pl.ds(0, 2), :, 0], ring_send.at[layer, 2])
        await_send(weight.at[layer, 0, :, 0], ring_send.at[layer, 3])
        await_send(weight.at[layer, :, :, 0], ring_send.at[layer, 4])

        @pl.when(layer % SECTIONS != z)
        def _():
            await_send(packed_all.at[layer], packed_send.at[layer])
            await_send(pairs_all.at[layer], pair_send.at[layer])

    loop(0, LAYERS, sent_layer)
    for v in range(2):
        def sent_line(s):
            await_send(weight.at[0, 0, 0, 0], zw_right.at[v, s])
            await_send(gains.at[0], zg_right.at[v, s])

            @pl.when(s <= 6)
            def _():
                await_send(weight.at[0, 0, 0, 0], zw_left.at[v, s])
                await_send(gains.at[0], zg_left.at[v, s])

        loop(0, 8, sent_line)

    def sent_plane(k):
        to = (d + k) % GROUPS
        await_send(half_out.at[to], half_send.at[to])
        await_send(home_out.at[to], home_send.at[to])

    def sent_sections(k):
        to = (z + k) % SECTIONS
        await_send(rows_out.at[to], rows_send.at[to])
        await_send(back_out.at[to], back_send.at[to])

    loop(1, GROUPS, sent_plane)
    loop(1, SECTIONS, sent_sections)

    def await_chip(k):
        at = (chip + k) % (GROUPS // 2)
        await_recv(chip_in.at[at], chip_recv.at[at])
        to = (chip + k) % (GROUPS // 2)
        await_send(chip_terms.at[to], chip_send.at[to])

    loop(1, GROUPS // 2, await_chip)
    for v in range(2):
        total = jnp.zeros((PART, 2 * HEAD), F32)
        for k in range(GROUPS // 2):
            total = total + chip_in[k, v].astype(F32)
        key_out_ref[v] = total[:, :HEAD]
        value_out_ref[v] = total[:, HEAD:]


def run_whole(source, lane_route, last, cosine, sine, gain, key_weight, value_weight):
    whole = pl.BlockSpec(memory_space=pltpu.VMEM)
    remote = pl.BlockSpec(memory_space=pl.ANY)
    dma = pltpu.SemaphoreType.DMA
    small = pltpu.VMEM((SECTIONS, ROWS, HEAD), F32)
    large = pltpu.VMEM((GROUPS, ROWS, HEAD), F32)
    chips = GROUPS // 2
    return pl.pallas_call(
        whole_kernel,
        out_shape=(
            jax.ShapeDtypeStruct((TILE, HEAD), BF16),
            jax.ShapeDtypeStruct((2, PART, HEAD), F32),
            jax.ShapeDtypeStruct((2, PART, HEAD), F32),
        ),
        in_specs=[whole] * 6 + [remote] * 2,
        out_specs=(whole, whole, whole),
        scratch_shapes=[
            pltpu.VMEM((LAYERS, SIDE, SIDE, 2, PART, 2 * HEAD), BF16),
            pltpu.VMEM((LAYERS, HEADS, HEAD), F32),
            pltpu.VMEM((TILE, HEAD), F32),
            pltpu.VMEM((LAYERS, TILE, HEAD), F32),
            pltpu.VMEM((LAYERS, TILE, HEAD), BF16),
            pltpu.VMEM((LAYERS, 2, ROWS, HEAD), BF16),
            pltpu.VMEM((LAYERS, ROWS, TILE), F32),
            pltpu.VMEM((LAYERS, ROWS, 1), F32),
            pltpu.VMEM((ROWS, TILE), F32),
            pltpu.VMEM((2, ROWS, HEAD), F32),
            pltpu.VMEM((LAYERS, 2 * ROWS, FEATURES // 2), BF16),
            pltpu.VMEM((2, SECTIONS, 2 * ROWS, FEATURES // 2), BF16),
            pltpu.VMEM((LAYERS, ROWS, 2 * HEAD), F32),
            pltpu.VMEM((2, SECTIONS, ROWS, 2 * HEAD), F32),
            pltpu.VMEM((chips, 2, 2, PART, 2 * HEAD), BF16),
            pltpu.VMEM((chips, 2, PART, 2 * HEAD), BF16),
            pltpu.VMEM((chips, 2, PART, 2 * HEAD), BF16),
            pltpu.VMEM((chips, 2, PART, 2 * HEAD), BF16),
            pltpu.VMEM((2 * TILE, TILE), BF16),
            pltpu.VMEM((2 * TILE, TILE), BF16),
            large, large, small, small, small, small, large, large,
            dma((2, 2)),
            dma((LAYERS,)), dma((2, 8)), dma((2, 8)),
            dma((LAYERS,)), dma((2, 8)), dma((2, 8)),
            dma((LAYERS, 5)), dma((LAYERS, 9)),
            dma((LAYERS,)), dma((2, SECTIONS)), dma((LAYERS,)), dma((2, SECTIONS)),
            dma((GROUPS,)), dma((GROUPS,)), dma((SECTIONS,)), dma((SECTIONS,)),
            dma((SECTIONS,)), dma((SECTIONS,)), dma((GROUPS,)), dma((GROUPS,)),
            dma(()), dma(()), dma((chips,)), dma((chips,)),
        ],
        compiler_params=pltpu.CompilerParams(
            collective_id=0, has_side_effects=True, vmem_limit_bytes=56 * 2**20),
    )(source, lane_route, last, cosine, sine, gain, key_weight, value_weight)


def body(hidden, lengths, route, gain, key_weight, value_weight, cotangent):
    section = lax.axis_index("pipe")
    half_rows = ROWS // 2
    half_count = 2 * lengths.shape[0]

    document, position = document_positions(lengths, ROWS)
    lane = jnp.arange(HEAD, dtype=jnp.int32)[None, :]
    slot = jnp.repeat(jnp.arange(half_count, dtype=jnp.int32), half_rows)[:, None]
    tags = jnp.where(
        lane < HEAD // 4, document.reshape(TILE, 1),
        jnp.where(lane < HEAD // 2, position.reshape(TILE, 1), slot))
    source = jnp.concatenate([hidden, tags.astype(BF16)], axis=0)
    lane_route = jnp.tile(jnp.repeat(route.reshape(half_count), half_rows), 2)[None, :]
    half = HEAD // 2
    frequency = ROPE_BASE ** (-(jnp.arange(half, dtype=F32) * 2.0 / HEAD))
    angles = jnp.arange(ROWS, dtype=F32)[:, None] * frequency
    cosine, sine = jnp.cos(angles), jnp.sin(angles)
    cosine = jnp.concatenate([cosine, cosine], axis=-1)
    sine = jnp.concatenate([-sine, sine], axis=-1)
    last = lax.dynamic_slice_in_dim(cotangent, section * ROWS, ROWS, 0)
    last = jnp.swapaxes(last.reshape(ROWS, HEADS, HEAD), 0, 1).reshape(TILE, HEAD).astype(F32)
    return run_whole(
        source, lane_route, last, cosine, sine, gain.reshape(2, HEADS, HEAD),
        key_weight, value_weight)


def solution(mesh):
    placed = (
        P("dp", "pipe"),
        P("dp", None),
        P("dp", None),
        P("pipe", None),
        P("pipe", None, None),
        P("pipe", None, None),
        P("dp", None),
    )
    return jax.shard_map(
        body,
        mesh=mesh,
        in_specs=placed,
        out_specs=(P("dp", "pipe"), P("pipe", "dp", None), P("pipe", "dp", None)),
        check_vma=False,
    )
```

```python
import math

import jax
import jax.numpy as jnp
from jax import lax
from jax.experimental import pallas as pl
from jax.experimental.pallas import tpu as pltpu
from jax.sharding import PartitionSpec as P

ROPE_BASE = 500000.0
EPSILON = 1e-05
NEGATIVE = -1e30
HEADS = 16
ROWS = 8
HEAD = 128
SECTIONS = 16
GROUPS = 32
LAYERS = 32
SIDE = 4
PART = 64
TILE = HEADS * ROWS
FEATURES = HEADS * HEAD
F32 = jnp.float32
BF16 = jnp.bfloat16
MESH = pl.DeviceIdType.MESH


def dot(a, b, over_a, over_b):
    return lax.dot_general(
        a, b, (((over_a,), (over_b,)), ((), ())), preferred_element_type=F32
    )


def swap_halves(flat):
    return pltpu.roll(flat, HEAD // 2, 1)


def turn(flat, cosine, sine):
    return flat * cosine + swap_halves(flat) * sine


def unturn(flat, cosine, sine):
    return flat * cosine - swap_halves(flat) * sine


def side_by_side(flat):
    return jnp.concatenate([flat[ROWS * h:ROWS * (h + 1)] for h in range(HEADS)], axis=1)


def stacked(wide):
    return jnp.concatenate([wide[:, HEAD * h:HEAD * (h + 1)] for h in range(HEADS)], axis=0)


def row_mean(flat):
    total = jnp.sum(flat.reshape(HEADS, ROWS, HEAD), axis=0)
    return jnp.sum(total, axis=-1, keepdims=True) * (1.0 / (HEADS * HEAD))


def over_heads(rows):
    return jnp.broadcast_to(rows[None], (HEADS, ROWS, rows.shape[-1])).reshape(
        HEADS * ROWS, rows.shape[-1]
    )


def gain_rows(gain):
    return jnp.broadcast_to(gain[:, None, :], (HEADS, ROWS, HEAD)).reshape(HEADS * ROWS, HEAD)


def whole_kernel(
    hidden_ref, lengths_ref, route_ref, gain_ref, key_ref, value_ref, cotangent_ref,
    grad_ref, key_out_ref, value_out_ref,
    weight, gains, current, saved, saved_queries, saved_keys, saved_weights, saved_scale, bias, turns,
    packed_all, packed_in, pairs_all, pairs_in, terms, twin_in, chip_terms, chip_in,
    sorting, placing, half_out, half_in, rows_out, rows_in, back_out, back_in, home_out, home_in,
    last, last_sem, own_sem, zw_recv, zw_right, zw_left, zg_recv, zg_right, zg_left,
    ring_send, ring_recv, packed_send, packed_recv, pair_send, pair_recv,
    half_send, half_recv, rows_send, rows_recv, back_send, back_recv, home_send, home_recv,
    twin_send, twin_recv, chip_send, chip_recv,
):
    z = lax.axis_index("pipe")
    d = lax.axis_index("dp")
    core = d % 2
    chip = d // 2
    px, py = chip // SIDE, chip % SIDE
    twin = chip * 2 + 1 - core
    z_next, z_before = (z + 1) % SECTIONS, (z + SECTIONS - 1) % SECTIONS

    def remote(src, dst, send, recv, to_z, to_d):
        return pltpu.make_async_remote_copy(
            src_ref=src, dst_ref=dst, send_sem=send, recv_sem=recv,
            device_id={"pipe": to_z, "dp": to_d}, device_id_type=MESH,
        )

    def await_recv(ref, sem):
        remote(ref, ref, sem, sem, z, twin).wait_recv()

    def await_send(ref, sem):
        remote(ref, ref, sem, sem, z, twin).wait_send()

    def loop(low, high, run):
        lax.fori_loop(low, high, lambda i, c: (run(i), c)[1], 0)

    owned = []
    for v in range(2):
        own = weight.at[v * SECTIONS + z]
        owned.append(pltpu.make_async_copy(
            key_ref.at[v], own.at[:, :, :, :, pl.ds(0, HEAD)], own_sem.at[v, 0]))
        owned.append(pltpu.make_async_copy(
            value_ref.at[v], own.at[:, :, :, :, pl.ds(HEAD, HEAD)], own_sem.at[v, 1]))
    for copy in owned:
        copy.start()
    upstream_rows = pl.ds(pl.multiple_of(z // 2 * 2 * ROWS, 2 * ROWS), 2 * ROWS)
    last_copy = pltpu.make_async_copy(cotangent_ref.at[upstream_rows, :], last, last_sem)
    last_copy.start()
    for v in range(2):
        gains[z, v] = jnp.concatenate(
            [gain_ref[v:v + 1, HEAD * h:HEAD * (h + 1)] for h in range(HEADS)], axis=0)

    row = lax.broadcasted_iota(jnp.int32, (2 * TILE, 2 * TILE), 0)
    col = lax.broadcasted_iota(jnp.int32, (2 * TILE, 2 * TILE), 1)
    kind_row = (col // TILE) * (ROWS // 2) + col % (ROWS // 2)
    micro = lax.broadcasted_iota(jnp.int32, (SECTIONS, 2 * TILE), 0)
    lane = lax.broadcasted_iota(jnp.int32, (SECTIONS, 2 * TILE), 1) % TILE
    spread_out = jnp.where(micro == lane // ROWS, 1.0, 0.0).astype(BF16)
    lane_route = dot(route_ref[...].astype(F32).astype(BF16), spread_out, 1, 0)
    leading = lane[0:1] // (ROWS // 2) % 2 == 0
    lane_route = jnp.where(leading, lane_route[0:1], lane_route[1:2])
    chosen = (lane_route == (row // ROWS).astype(F32)) & (row % ROWS == kind_row)
    sort = jnp.where(chosen, 1.0, 0.0).astype(BF16)
    sorting[...] = sort[:, :TILE]
    row = lax.broadcasted_iota(jnp.int32, (TILE, SECTIONS), 0)
    col = lax.broadcasted_iota(jnp.int32, (TILE, SECTIONS), 1)
    spread_out = jnp.where(row // ROWS == col, 1.0, 0.0).astype(BF16)
    row_lengths = dot(spread_out, lengths_ref[...].astype(F32).astype(BF16), 1, 1)
    row = lax.broadcasted_iota(jnp.int32, (TILE, HEAD), 0)
    lane = lax.broadcasted_iota(jnp.int32, (TILE, HEAD), 1)
    at = (row % ROWS).astype(F32)
    ends = [jnp.broadcast_to(row_lengths[:, 0:1], (TILE, HEAD))]
    for k in range(1, row_lengths.shape[1] - 1):
        ends.append(ends[-1] + row_lengths[:, k:k + 1])
    document = jnp.zeros((TILE, HEAD), F32)
    opening = jnp.zeros((TILE, HEAD), F32)
    for end in ends:
        document = document + jnp.where(at >= end, 1.0, 0.0)
        opening = jnp.where(at >= end, end, opening)
    slots = (row // (ROWS // 2)).astype(F32)
    tags = jnp.where(lane < HEAD // 4, document, jnp.where(lane < HEAD // 2, at - opening, slots))
    source = jnp.concatenate([hidden_ref[...], tags.astype(BF16)], axis=0)
    half_out[...] = dot(sort, source, 1, 0).reshape(GROUPS, ROWS, HEAD)
    half_in[d] = half_out[d]

    barrier = pltpu.get_barrier_semaphore()

    def greet_plane(k):
        pl.semaphore_signal(
            barrier, inc=1, device_id={"pipe": z, "dp": (d + k) % GROUPS}, device_id_type=MESH)

    def greet_line(k):
        pl.semaphore_signal(
            barrier, inc=1, device_id={"pipe": (z + k) % SECTIONS, "dp": d}, device_id_type=MESH)

    loop(1, GROUPS, greet_plane)
    loop(1, SECTIONS, greet_line)
    pl.semaphore_wait(barrier, GROUPS + SECTIONS - 2)

    def send_half(k):
        to = (d + k) % GROUPS
        remote(half_out.at[to], half_in.at[d], half_send.at[to], half_recv.at[d], z, to).start()

    for copy in owned:
        copy.wait()

    def row_of(layer, e):
        return weight.at[layer, :, py, core] if e == 0 else weight.at[layer, px, :, core]

    def line_step(v, s):
        on_left = (z + SECTIONS - s) % SECTIONS
        on_right = (z + s) % SECTIONS
        left_rows = row_of(v * SECTIONS + on_left, 0)
        right_rows = row_of(v * SECTIONS + on_right, 1)

        @pl.when(s >= 1)
        def _():
            await_recv(left_rows, zw_recv.at[v, on_left])

        @pl.when(s <= 7)
        def _():
            remote(left_rows, left_rows, zw_right.at[v, s], zw_recv.at[v, on_left], z_next, d).start()

        @pl.when((s >= 1) & (s <= 7))
        def _():
            await_recv(right_rows, zw_recv.at[v, on_right])

        @pl.when(s <= 6)
        def _():
            remote(right_rows, right_rows, zw_left.at[v, s], zw_recv.at[v, on_right], z_before, d).start()

    def gain_step(s):
        on_left = (z + SECTIONS - s) % SECTIONS
        on_right = (z + s) % SECTIONS

        @pl.when(s >= 1)
        def _():
            await_recv(gains.at[on_left], zg_recv.at[on_left])

        @pl.when(s <= 7)
        def _():
            line = gains.at[on_left]
            remote(line, line, zg_right.at[s], zg_recv.at[on_left], z_next, d).start()

        @pl.when((s >= 1) & (s <= 7))
        def _():
            await_recv(gains.at[on_right], zg_recv.at[on_right])

        @pl.when(s <= 6)
        def _():
            line = gains.at[on_right]
            remote(line, line, zg_left.at[s], zg_recv.at[on_right], z_before, d).start()

    line_step(0, 0)
    gain_step(0)
    loop(1, GROUPS, send_half)

    def await_half(k):
        at = (d + k) % GROUPS
        await_recv(half_in.at[at], half_recv.at[at])

    def send_rows(k):
        to = (z + k) % SECTIONS
        remote(rows_out.at[to], rows_in.at[z], rows_send.at[to], rows_recv.at[z], to, d).start()

    def place_halves():
        loop(1, GROUPS, await_half)
        arrived = half_in[...]
        slot = jnp.broadcast_to(arrived[:, 4:5, HEAD // 2:HEAD // 2 + 1], (GROUPS, ROWS, 1))
        slot = slot.reshape(2 * TILE, 1)
        arrived = arrived.reshape(2 * TILE, HEAD).astype(BF16)
        row = lax.broadcasted_iota(jnp.int32, (2 * TILE, TILE), 0) % ROWS
        col = lax.broadcasted_iota(jnp.int32, (2 * TILE, TILE), 1)
        same = slot == (col // (ROWS // 2)).astype(F32)
        place = jnp.where(same & (row == col % (ROWS // 2)), 1.0, 0.0).astype(BF16)
        place_tags = jnp.where(same & (row == col % (ROWS // 2) + ROWS // 2), 1.0, 0.0).astype(BF16)
        placing[...] = place
        rows_out[...] = dot(place, arrived, 0, 0).reshape(SECTIONS, ROWS, HEAD)
        home_out[pl.ds(0, SECTIONS)] = dot(place_tags, arrived, 0, 0).reshape(SECTIONS, ROWS, HEAD)
        rows_in[z] = rows_out[z]

        loop(1, SECTIONS, send_rows)

        tags = home_out[z]
        document = jnp.broadcast_to(tags[:, 0:1], (ROWS, TILE))
        position = jnp.broadcast_to(tags[:, HEAD // 4:HEAD // 4 + 1], (ROWS, TILE))
        lane = lax.broadcasted_iota(jnp.int32, (ROWS, TILE), 1) % ROWS
        mine = lane == lax.broadcasted_iota(jnp.int32, (ROWS, TILE), 0)
        query_document = jnp.sum(jnp.where(mine, document, 0.0), axis=0, keepdims=True)
        query_position = jnp.sum(jnp.where(mine, position, 0.0), axis=0, keepdims=True)
        allowed = (document == query_document) & (position <= query_position)
        bias[...] = jnp.where(allowed, 0.0, NEGATIVE)
        lane = lax.broadcasted_iota(jnp.int32, (ROWS, HEAD), 1)
        power = (lane % (HEAD // 2)).astype(F32) * (-2.0 / HEAD)
        angles = position * jnp.exp(power * math.log(ROPE_BASE))
        sine = jnp.sin(angles)
        turns[0] = jnp.cos(angles)
        turns[1] = jnp.where(lane < HEAD // 2, -sine, sine)

    def await_rows(k):
        at = (z + k) % SECTIONS
        await_recv(rows_in.at[at], rows_recv.at[at])

    def take_rows():
        loop(1, SECTIONS, await_rows)
        current[...] = rows_in[...].reshape(TILE, HEAD)

    def partner(j):
        return (z + jnp.where(j % 2 == 1, (j + 1) // 2, SECTIONS - j // 2)) % SECTIONS

    def send_packed(v, j):
        to = partner(j)
        remote(packed_all.at[v * SECTIONS + to], packed_in.at[v, z],
               packed_send.at[v, to], packed_recv.at[v, z], to, d).start()

    def send_pairs(v, j):
        to = partner(j)
        remote(pairs_all.at[v * SECTIONS + to], pairs_in.at[v, z],
               pair_send.at[v, to], pair_recv.at[v, z], to, d).start()

    def forward(layer):
        cosine, sine = turns[0], turns[1]
        cosine_all, sine_all = over_heads(cosine), over_heads(sine)
        x = current[...]
        saved[layer] = x
        scale = lax.rsqrt(row_mean(x * x) + EPSILON)
        saved_scale[layer] = scale
        normed = x * over_heads(scale) * gain_rows(gains[layer % SECTIONS, layer // SECTIONS])
        wide = side_by_side(normed)
        pre = dot(wide.astype(BF16), weight[layer].reshape(FEATURES, 2 * HEAD), 1, 0)
        packed = jnp.concatenate(
            [wide[:, :FEATURES // 2], wide[:, FEATURES // 2:]], axis=0).astype(BF16)
        packed_all[layer] = packed
        owner, v = layer % SECTIONS, layer // SECTIONS

        @pl.when(owner == z)
        def _():
            packed_in[v, z] = packed

        keys = turn(pre[:, :HEAD], cosine, sine).astype(BF16)
        values = pre[:, HEAD:].astype(BF16)
        queries = turn(normed, cosine_all, sine_all).astype(BF16)
        scores = dot(keys, queries, 1, 1) * HEAD ** (-0.5) + bias[...]
        raised = jnp.exp(scores - jnp.max(scores, axis=0, keepdims=True))
        weights = raised / jnp.sum(raised, axis=0, keepdims=True)
        saved_queries[layer] = queries
        saved_keys[layer, 0] = keys
        saved_keys[layer, 1] = values
        saved_weights[layer] = weights
        current[...] = x + dot(weights.astype(BF16), values, 0, 0)

    def rows_at(layer, e, at, rows):
        if e == 0:
            return weight.at[layer, :, at, core, rows, :]
        return weight.at[layer, at, :, core, rows, :]

    def device_by(e, by):
        if e == 0:
            return (px * SIDE + (py + by) % SIDE) * 2 + core
        return (((px + by) % SIDE) * SIDE + py) * 2 + core

    def around(e, by):
        return ((py if e == 0 else px) + by) % SIDE

    every, low, high = pl.ds(0, PART), pl.ds(0, PART // 2), pl.ds(PART // 2, PART // 2)

    def stage_one(layer, e):
        line = rows_at(layer, e, around(e, 0), every)
        remote(line, line, ring_send.at[layer, 0], ring_recv.at[layer, 0], z, device_by(e, 1)).start()
        remote(line, line, ring_send.at[layer, 0], ring_recv.at[layer, 1], z, device_by(e, 3)).start()

    def stage_two(layer, e):
        left, right = around(e, 3), around(e, 1)
        await_recv(rows_at(layer, e, left, every), ring_recv.at[layer, 0])
        part = rows_at(layer, e, left, low)
        remote(part, part, ring_send.at[layer, 1], ring_recv.at[layer, 2], z, device_by(e, 1)).start()
        await_recv(rows_at(layer, e, right, every), ring_recv.at[layer, 1])
        part = rows_at(layer, e, right, high)
        remote(part, part, ring_send.at[layer, 1], ring_recv.at[layer, 3], z, device_by(e, 3)).start()

    def stage_three(layer, e):
        far = around(e, 2)
        await_recv(rows_at(layer, e, far, low), ring_recv.at[layer, 2])
        await_recv(rows_at(layer, e, far, high), ring_recv.at[layer, 3])
        half = weight.at[layer, :, :, core]
        remote(half, half, ring_send.at[layer, 2], ring_recv.at[layer, 4], z, twin).start()

    def stage_four(layer, e):
        await_recv(weight.at[layer, :, :, 1 - core], ring_recv.at[layer, 4])

    def turn_of(t):
        @pl.when((t >= 1) & (t <= 8))
        def _():
            line_step(0, t)
            gain_step(t)

        @pl.when((t <= 7) & (t % 2 == 1))
        def _():
            line_step(1, t // 2)

        @pl.when((t >= 8) & (t <= 12))
        def _():
            line_step(1, t - 4)

        for late, stage in ((0, stage_one), (1, stage_two), (2, stage_three), (3, stage_four)):
            v = jnp.where(t - late <= 8, 0, 1)
            s = t - late - 8 * v

            @pl.when((s >= 1) & (s <= 8))
            def _():
                stage(v * SECTIONS + (z + SECTIONS - s) % SECTIONS, 0)

            @pl.when((s >= 1) & (s <= 7))
            def _():
                stage(v * SECTIONS + (z + s) % SECTIONS, 1)

        @pl.when(t == 3)
        def _():
            place_halves()

        @pl.when(t == 11)
        def _():
            take_rows()

        @pl.when((t >= 11) & (t <= 14))
        def _():
            loop(4 * (t - 11), 4 * (t - 11) + 4, forward)

        @pl.when(t >= 15)
        def _():
            for k in range(1, 4):
                send_packed(0, 3 * (t - 15) + k)

    loop(1, 20, turn_of)

    loop(SECTIONS, LAYERS, forward)

    last_copy.wait()
    both = last[...].astype(F32)
    current[...] = stacked(jnp.where(z % 2 == 0, both[:ROWS], both[ROWS:]))

    def backward(step):
        layer = LAYERS - 1 - step
        cosine, sine = turns[0], turns[1]
        cosine_all, sine_all = over_heads(cosine), over_heads(sine)
        upstream = current[...]
        rounded = upstream.astype(BF16)
        keys = saved_keys[layer, 0]
        values = saved_keys[layer, 1]
        weights = saved_weights[layer]
        d_weights = dot(values, rounded, 1, 1).astype(BF16).astype(F32)
        d_values = dot(weights.astype(BF16), rounded, 1, 0).astype(BF16).astype(F32)
        inner = jnp.sum(d_weights * weights, axis=0, keepdims=True)
        d_scores = (weights * (d_weights - inner) * HEAD ** (-0.5)).astype(BF16)
        d_queries = dot(d_scores, keys, 0, 0).astype(BF16).astype(F32)
        d_keys = dot(d_scores, saved_queries[layer], 1, 0).astype(BF16).astype(F32)
        d_key_pre = unturn(d_keys, cosine, sine)
        pair = jnp.concatenate([d_key_pre, d_values], axis=1).astype(BF16)
        pair_rows = jnp.concatenate([d_key_pre, d_values], axis=0).astype(BF16)
        pairs_all[layer] = pair_rows
        owner, v = layer % SECTIONS, layer // SECTIONS

        @pl.when(owner == z)
        def _():
            pairs_in[v, z] = pair_rows

        d_packed = stacked(
            dot(pair, weight[layer].reshape(FEATURES, 2 * HEAD), 1, 1))
        d_normed = unturn(d_queries, cosine_all, sine_all) + d_packed
        x = saved[layer]
        scale = saved_scale[layer]
        scaled = d_normed * gain_rows(gains[layer % SECTIONS, layer // SECTIONS])
        pull = row_mean(scaled * x) * scale * scale * scale
        current[...] = upstream + scaled * over_heads(scale) - x * over_heads(pull)

    def terms_of(v):
        def await_rows_of(k):
            at = (z + k) % SECTIONS
            await_recv(packed_in.at[v, at], packed_recv.at[v, at])
            await_recv(pairs_in.at[v, at], pair_recv.at[v, at])

        loop(1, SECTIONS, await_rows_of)
        pair = pairs_in[v].astype(F32)
        pair = jnp.concatenate([pair[:, :ROWS], pair[:, ROWS:]], axis=2)
        nothing = jnp.zeros_like(pair)
        upper = jnp.concatenate([pair, nothing], axis=1).reshape(2 * TILE, 2 * HEAD)
        lower = jnp.concatenate([nothing, pair], axis=1).reshape(2 * TILE, 2 * HEAD)
        both = jnp.concatenate([upper, lower], axis=1).astype(BF16)
        product = dot(packed_in[v].reshape(2 * TILE, FEATURES // 2), both, 0, 0).astype(BF16)
        for g in range(GROUPS):
            rows = product[PART * (g % 16):PART * (g % 16 + 1)]
            terms[v, g // 2, g % 2] = rows[:, 2 * HEAD * (g // 16):2 * HEAD * (g // 16 + 1)]
        remote(terms.at[v, :, 1 - core], twin_in.at[v],
               twin_send.at[v], twin_recv.at[v], z, twin).start()

    def send_chips(v):
        await_recv(twin_in.at[v], twin_recv.at[v])
        chip_terms[v] = (terms[v, :, core].astype(F32) + twin_in[v].astype(F32)).astype(BF16)

        def send_chip(k):
            to = (chip + k) % (GROUPS // 2)
            remote(chip_terms.at[v, to], chip_in.at[v, chip],
                   chip_send.at[v, to], chip_recv.at[v, chip], z, 2 * to + core).start()

        loop(1, GROUPS // 2, send_chip)
        chip_in[v, chip] = chip_terms[v, chip]

    def backward_step(j):
        backward(j)

        @pl.when((j >= 1) & (j < SECTIONS))
        def _():
            send_packed(1, j)

        @pl.when((j >= SECTIONS) & (j < SECTIONS + 8))
        def _():
            send_pairs(1, 2 * (j - SECTIONS) + 1)

        @pl.when((j >= SECTIONS) & (j < SECTIONS + 7))
        def _():
            send_pairs(1, 2 * (j - SECTIONS) + 2)

        @pl.when(j == 27)
        def _():
            terms_of(1)

        @pl.when(j == 30)
        def _():
            send_chips(1)

    loop(0, LAYERS, backward_step)
    loop(1, SECTIONS, lambda j: send_pairs(0, j))

    back_out[...] = current[...].astype(BF16).astype(F32).reshape(SECTIONS, ROWS, HEAD)
    back_in[z] = back_out[z]

    def send_back(k):
        to = (z + k) % SECTIONS
        remote(back_out.at[to], back_in.at[z], back_send.at[to], back_recv.at[z], to, d).start()

    loop(1, SECTIONS, send_back)
    terms_of(0)

    def await_back(k):
        at = (z + k) % SECTIONS
        await_recv(back_in.at[at], back_recv.at[at])

    loop(1, SECTIONS, await_back)
    mine = back_in[...].reshape(TILE, HEAD).astype(BF16)
    home_out[...] = dot(placing[...], mine, 1, 0).reshape(GROUPS, ROWS, HEAD)
    home_in[d] = home_out[d]

    def send_home(k):
        to = (d + k) % GROUPS
        remote(home_out.at[to], home_in.at[d], home_send.at[to], home_recv.at[d], z, to).start()

    loop(1, GROUPS, send_home)
    send_chips(0)

    def await_home(k):
        at = (d + k) % GROUPS
        await_recv(home_in.at[at], home_recv.at[at])

    loop(1, GROUPS, await_home)
    arrived = home_in[...].reshape(2 * TILE, HEAD).astype(BF16)
    grad_ref[...] = dot(sorting[...], arrived, 0, 0).astype(BF16)

    def sent_layer(layer):
        @pl.when(layer % SECTIONS != z)
        def _():
            await_send(weight.at[layer, pl.ds(0, 2), :, 0], ring_send.at[layer, 0])
            await_send(weight.at[layer, 0, :, 0], ring_send.at[layer, 1])
            await_send(weight.at[layer, :, :, 0], ring_send.at[layer, 2])
            await_send(packed_all.at[layer], packed_send.at[layer // SECTIONS, layer % SECTIONS])
            await_send(pairs_all.at[layer], pair_send.at[layer // SECTIONS, layer % SECTIONS])

    loop(0, LAYERS, sent_layer)

    def sent_line(s):
        await_send(gains.at[0], zg_right.at[s])
        for v in range(2):
            await_send(row_of(0, 0), zw_right.at[v, s])

        @pl.when(s <= 6)
        def _():
            await_send(gains.at[0], zg_left.at[s])
            for v in range(2):
                await_send(row_of(0, 1), zw_left.at[v, s])

    loop(0, 8, sent_line)

    def sent_plane(k):
        to = (d + k) % GROUPS
        await_send(half_out.at[to], half_send.at[to])
        await_send(home_out.at[to], home_send.at[to])

    def sent_sections(k):
        to = (z + k) % SECTIONS
        await_send(rows_out.at[to], rows_send.at[to])
        await_send(back_out.at[to], back_send.at[to])

    loop(1, GROUPS, sent_plane)
    loop(1, SECTIONS, sent_sections)

    for v in range(2):
        await_send(twin_in.at[v], twin_send.at[v])

        def await_chip(k):
            at = (chip + k) % (GROUPS // 2)
            await_recv(chip_in.at[v, at], chip_recv.at[v, at])
            await_send(chip_terms.at[v, at], chip_send.at[v, at])

        loop(1, GROUPS // 2, await_chip)
        total = jnp.zeros((PART, 2 * HEAD), F32)
        for k in range(GROUPS // 2):
            total = total + chip_in[v, k].astype(F32)
        key_out_ref[v] = total[:, :HEAD]
        value_out_ref[v] = total[:, HEAD:]


def run_whole(hidden, lengths, route, gain, key_weight, value_weight, cotangent):
    whole = pl.BlockSpec(memory_space=pltpu.VMEM)
    remote = pl.BlockSpec(memory_space=pl.ANY)
    dma = pltpu.SemaphoreType.DMA
    small = pltpu.VMEM((SECTIONS, ROWS, HEAD), F32)
    large = pltpu.VMEM((GROUPS, ROWS, HEAD), F32)
    chips = GROUPS // 2
    return pl.pallas_call(
        whole_kernel,
        out_shape=(
            jax.ShapeDtypeStruct((TILE, HEAD), BF16),
            jax.ShapeDtypeStruct((2, PART, HEAD), F32),
            jax.ShapeDtypeStruct((2, PART, HEAD), F32),
        ),
        in_specs=[whole] * 4 + [remote] * 3,
        out_specs=(whole, whole, whole),
        scratch_shapes=[
            pltpu.VMEM((LAYERS, SIDE, SIDE, 2, PART, 2 * HEAD), BF16),
            pltpu.VMEM((SECTIONS, 2, HEADS, HEAD), F32),
            pltpu.VMEM((TILE, HEAD), F32),
            pltpu.VMEM((LAYERS, TILE, HEAD), F32),
            pltpu.VMEM((LAYERS, TILE, HEAD), BF16),
            pltpu.VMEM((LAYERS, 2, ROWS, HEAD), BF16),
            pltpu.VMEM((LAYERS, ROWS, TILE), F32),
            pltpu.VMEM((LAYERS, ROWS, 1), F32),
            pltpu.VMEM((ROWS, TILE), F32),
            pltpu.VMEM((2, ROWS, HEAD), F32),
            pltpu.VMEM((LAYERS, 2 * ROWS, FEATURES // 2), BF16),
            pltpu.VMEM((2, SECTIONS, 2 * ROWS, FEATURES // 2), BF16),
            pltpu.VMEM((LAYERS, 2 * ROWS, HEAD), BF16),
            pltpu.VMEM((2, SECTIONS, 2 * ROWS, HEAD), BF16),
            pltpu.VMEM((2, chips, 2, PART, 2 * HEAD), BF16),
            pltpu.VMEM((2, chips, PART, 2 * HEAD), BF16),
            pltpu.VMEM((2, chips, PART, 2 * HEAD), BF16),
            pltpu.VMEM((2, chips, PART, 2 * HEAD), BF16),
            pltpu.VMEM((2 * TILE, TILE), BF16),
            pltpu.VMEM((2 * TILE, TILE), BF16),
            large, large, small, small, small, small, large, large,
            pltpu.VMEM((2 * ROWS, FEATURES), BF16),
            dma(()), dma((2, 2)),
            dma((2, SECTIONS)), dma((2, 8)), dma((2, 8)),
            dma((SECTIONS,)), dma((8,)), dma((8,)),
            dma((LAYERS, 3)), dma((LAYERS, 5)),
            dma((2, SECTIONS)), dma((2, SECTIONS)), dma((2, SECTIONS)), dma((2, SECTIONS)),
            dma((GROUPS,)), dma((GROUPS,)), dma((SECTIONS,)), dma((SECTIONS,)),
            dma((SECTIONS,)), dma((SECTIONS,)), dma((GROUPS,)), dma((GROUPS,)),
            dma((2,)), dma((2,)), dma((2, chips)), dma((2, chips)),
        ],
        compiler_params=pltpu.CompilerParams(
            collective_id=0, has_side_effects=True, vmem_limit_bytes=56 * 2**20),
    )(hidden, lengths, route, gain, key_weight, value_weight, cotangent)


def body(hidden, lengths, route, gain, key_weight, value_weight, cotangent):
    shares = (2, SIDE, SIDE, 2, PART, HEAD)
    return run_whole(
        hidden, lengths.T, route.T, gain,
        key_weight.reshape(shares), value_weight.reshape(shares), cotangent)


def solution(mesh):
    placed = (
        P("dp", "pipe"),
        P("dp", None),
        P("dp", None),
        P("pipe", None),
        P("pipe", None, None),
        P("pipe", None, None),
        P("dp", None),
    )
    return jax.shard_map(
        body,
        mesh=mesh,
        in_specs=placed,
        out_specs=(P("dp", "pipe"), P("pipe", "dp", None), P("pipe", "dp", None)),
        check_vma=False,
    )
```

```python
import math

import jax
import jax.numpy as jnp
from jax import lax
from jax.experimental import pallas as pl
from jax.experimental.pallas import tpu as pltpu
from jax.sharding import PartitionSpec as P

ROPE_BASE = 500000.0
EPSILON = 1e-05
NEGATIVE = -1e30
HEADS = 16
ROWS = 8
HEAD = 128
SECTIONS = 16
GROUPS = 32
LAYERS = 32
SIDE = 4
PART = 64
TILE = HEADS * ROWS
FEATURES = HEADS * HEAD
F32 = jnp.float32
BF16 = jnp.bfloat16
MESH = pl.DeviceIdType.MESH


def dot(a, b, over_a, over_b):
    return lax.dot_general(
        a, b, (((over_a,), (over_b,)), ((), ())), preferred_element_type=F32
    )


def swap_halves(flat):
    return pltpu.roll(flat, HEAD // 2, 1)


def turn(flat, cosine, sine):
    return flat * cosine + swap_halves(flat) * sine


def unturn(flat, cosine, sine):
    return flat * cosine - swap_halves(flat) * sine


def side_by_side(flat):
    return jnp.concatenate([flat[ROWS * h:ROWS * (h + 1)] for h in range(HEADS)], axis=1)


def stacked(wide):
    return jnp.concatenate([wide[:, HEAD * h:HEAD * (h + 1)] for h in range(HEADS)], axis=0)


def row_mean(flat):
    total = jnp.sum(flat.reshape(HEADS, ROWS, HEAD), axis=0)
    return jnp.sum(total, axis=-1, keepdims=True) * (1.0 / (HEADS * HEAD))


def over_heads(rows):
    return jnp.broadcast_to(rows[None], (HEADS, ROWS, rows.shape[-1])).reshape(
        HEADS * ROWS, rows.shape[-1]
    )


def gain_rows(gain):
    return jnp.broadcast_to(gain[:, None, :], (HEADS, ROWS, HEAD)).reshape(HEADS * ROWS, HEAD)


def whole_kernel(
    hidden_ref, lengths_ref, route_ref, gain_ref, key_ref, value_ref, cotangent_ref,
    grad_ref, key_out_ref, value_out_ref,
    weight, gains, current, saved, saved_queries, saved_keys, saved_weights, saved_scale, bias, turns,
    packed_all, packed_in, pairs_all, pairs_in, terms, twin_in, chip_terms, chip_in,
    sorting, placing, half_out, half_in, rows_out, rows_in, back_out, back_in, home_out, home_in,
    last, last_sem, own_sem, zw_recv, zw_right, zw_left, zg_recv, zg_right, zg_left,
    ring_send, ring_recv, packed_send, packed_recv, pair_send, pair_recv,
    half_send, half_recv, rows_send, rows_recv, back_send, back_recv, home_send, home_recv,
    twin_send, twin_recv, chip_send, chip_recv,
):
    z = lax.axis_index("pipe")
    d = lax.axis_index("dp")
    core = d % 2
    chip = d // 2
    px, py = chip // SIDE, chip % SIDE
    twin = chip * 2 + 1 - core
    z_next, z_before = (z + 1) % SECTIONS, (z + SECTIONS - 1) % SECTIONS

    def loop(low, high, run):
        lax.fori_loop(low, high, lambda i, c: (run(i), c)[1], 0)

    barrier = pltpu.get_barrier_semaphore()

    def greet_plane(k):
        pl.semaphore_signal(
            barrier, inc=1, device_id={"pipe": z, "dp": (d + k) % GROUPS}, device_id_type=MESH)

    def greet_line(k):
        pl.semaphore_signal(
            barrier, inc=1, device_id={"pipe": (z + k) % SECTIONS, "dp": d}, device_id_type=MESH)

    loop(1, GROUPS, greet_plane)
    loop(1, SECTIONS, greet_line)

    def remote(src, dst, send, recv, to_z, to_d):
        return pltpu.make_async_remote_copy(
            src_ref=src, dst_ref=dst, send_sem=send, recv_sem=recv,
            device_id={"pipe": to_z, "dp": to_d}, device_id_type=MESH,
        )

    def await_recv(ref, sem):
        remote(ref, ref, sem, sem, z, twin).wait_recv()

    def await_send(ref, sem):
        remote(ref, ref, sem, sem, z, twin).wait_send()

    owned = []
    for v in range(2):
        own = weight.at[v * SECTIONS + z]
        owned.append(pltpu.make_async_copy(
            key_ref.at[v], own.at[:, :, :, :, pl.ds(0, HEAD)], own_sem.at[v, 0]))
        owned.append(pltpu.make_async_copy(
            value_ref.at[v], own.at[:, :, :, :, pl.ds(HEAD, HEAD)], own_sem.at[v, 1]))
    for copy in owned:
        copy.start()
    upstream_rows = pl.ds(pl.multiple_of(z // 2 * 2 * ROWS, 2 * ROWS), 2 * ROWS)
    last_copy = pltpu.make_async_copy(cotangent_ref.at[upstream_rows, :], last, last_sem)
    last_copy.start()
    for v in range(2):
        gains[z, v] = jnp.concatenate(
            [gain_ref[v:v + 1, HEAD * h:HEAD * (h + 1)] for h in range(HEADS)], axis=0)

    row = lax.broadcasted_iota(jnp.int32, (2 * TILE, 2 * TILE), 0)
    col = lax.broadcasted_iota(jnp.int32, (2 * TILE, 2 * TILE), 1)
    kind_row = (col // TILE) * (ROWS // 2) + col % (ROWS // 2)
    micro = lax.broadcasted_iota(jnp.int32, (SECTIONS, 2 * TILE), 0)
    lane = lax.broadcasted_iota(jnp.int32, (SECTIONS, 2 * TILE), 1) % TILE
    spread_out = jnp.where(micro == lane // ROWS, 1.0, 0.0).astype(BF16)
    lane_route = dot(route_ref[...].astype(F32).astype(BF16), spread_out, 1, 0)
    leading = lane[0:1] // (ROWS // 2) % 2 == 0
    lane_route = jnp.where(leading, lane_route[0:1], lane_route[1:2])
    chosen = (lane_route == (row // ROWS).astype(F32)) & (row % ROWS == kind_row)
    sort = jnp.where(chosen, 1.0, 0.0).astype(BF16)
    sorting[...] = sort[:, :TILE]
    row = lax.broadcasted_iota(jnp.int32, (TILE, SECTIONS), 0)
    col = lax.broadcasted_iota(jnp.int32, (TILE, SECTIONS), 1)
    spread_out = jnp.where(row // ROWS == col, 1.0, 0.0).astype(BF16)
    row_lengths = dot(spread_out, lengths_ref[...].astype(F32).astype(BF16), 1, 1)
    row = lax.broadcasted_iota(jnp.int32, (TILE, HEAD), 0)
    lane = lax.broadcasted_iota(jnp.int32, (TILE, HEAD), 1)
    at = (row % ROWS).astype(F32)
    ends = [jnp.broadcast_to(row_lengths[:, 0:1], (TILE, HEAD))]
    for k in range(1, row_lengths.shape[1] - 1):
        ends.append(ends[-1] + row_lengths[:, k:k + 1])
    document = jnp.zeros((TILE, HEAD), F32)
    opening = jnp.zeros((TILE, HEAD), F32)
    for end in ends:
        document = document + jnp.where(at >= end, 1.0, 0.0)
        opening = jnp.where(at >= end, end, opening)
    slots = (row // (ROWS // 2)).astype(F32)
    tags = jnp.where(lane < HEAD // 4, document, jnp.where(lane < HEAD // 2, at - opening, slots))
    source = jnp.concatenate([hidden_ref[...], tags.astype(BF16)], axis=0)
    half_out[...] = dot(sort, source, 1, 0).reshape(GROUPS, ROWS, HEAD)
    half_in[d] = half_out[d]

    pl.semaphore_wait(barrier, GROUPS + SECTIONS - 2)

    def send_half(k):
        to = (d + k) % GROUPS
        remote(half_out.at[to], half_in.at[d], half_send, half_recv, z, to).start()

    for copy in owned:
        copy.wait()

    def row_of(layer, e):
        return weight.at[layer, :, py, core] if e == 0 else weight.at[layer, px, :, core]

    def line_step(v, s):
        on_left = (z + SECTIONS - s) % SECTIONS
        on_right = (z + s) % SECTIONS
        for q in range(SIDE):
            left = weight.at[v * SECTIONS + on_left, q, py, core]
            right = weight.at[v * SECTIONS + on_right, px, q, core]
            left_sem = zw_recv.at[v, on_left, q]
            right_sem = zw_recv.at[v, on_right, q]

            @pl.when(s >= 1)
            def _():
                await_recv(left, left_sem)

            @pl.when(s <= 7)
            def _():
                remote(left, left, zw_right.at[v], left_sem, z_next, d).start()

            @pl.when((s >= 1) & (s <= 7))
            def _():
                await_recv(right, right_sem)

            @pl.when(s <= 6)
            def _():
                remote(right, right, zw_left.at[v], right_sem, z_before, d).start()

    def gain_step(s):
        on_left = (z + SECTIONS - s) % SECTIONS
        on_right = (z + s) % SECTIONS

        @pl.when(s >= 1)
        def _():
            await_recv(gains.at[on_left], zg_recv.at[on_left])

        @pl.when(s <= 7)
        def _():
            line = gains.at[on_left]
            remote(line, line, zg_right, zg_recv.at[on_left], z_next, d).start()

        @pl.when((s >= 1) & (s <= 7))
        def _():
            await_recv(gains.at[on_right], zg_recv.at[on_right])

        @pl.when(s <= 6)
        def _():
            line = gains.at[on_right]
            remote(line, line, zg_left, zg_recv.at[on_right], z_before, d).start()

    line_step(0, 0)
    gain_step(0)
    loop(1, GROUPS, send_half)

    def send_rows(k):
        to = (z + k) % SECTIONS
        remote(rows_out.at[to], rows_in.at[z], rows_send, rows_recv, to, d).start()

    def place_halves():
        await_recv(half_in.at[pl.ds(0, GROUPS - 1)], half_recv)
        arrived = half_in[...]
        slot = jnp.broadcast_to(arrived[:, 4:5, HEAD // 2:HEAD // 2 + 1], (GROUPS, ROWS, 1))
        slot = slot.reshape(2 * TILE, 1)
        arrived = arrived.reshape(2 * TILE, HEAD).astype(BF16)
        row = lax.broadcasted_iota(jnp.int32, (2 * TILE, TILE), 0) % ROWS
        col = lax.broadcasted_iota(jnp.int32, (2 * TILE, TILE), 1)
        same = slot == (col // (ROWS // 2)).astype(F32)
        place = jnp.where(same & (row == col % (ROWS // 2)), 1.0, 0.0).astype(BF16)
        place_tags = jnp.where(same & (row == col % (ROWS // 2) + ROWS // 2), 1.0, 0.0).astype(BF16)
        placing[...] = place
        rows_out[...] = dot(place, arrived, 0, 0).reshape(SECTIONS, ROWS, HEAD)
        home_out[pl.ds(0, SECTIONS)] = dot(place_tags, arrived, 0, 0).reshape(SECTIONS, ROWS, HEAD)
        rows_in[z] = rows_out[z]

        loop(1, SECTIONS, send_rows)

        tags = home_out[z]
        document = jnp.broadcast_to(tags[:, 0:1], (ROWS, TILE))
        position = jnp.broadcast_to(tags[:, HEAD // 4:HEAD // 4 + 1], (ROWS, TILE))
        lane = lax.broadcasted_iota(jnp.int32, (ROWS, TILE), 1) % ROWS
        mine = lane == lax.broadcasted_iota(jnp.int32, (ROWS, TILE), 0)
        query_document = jnp.sum(jnp.where(mine, document, 0.0), axis=0, keepdims=True)
        query_position = jnp.sum(jnp.where(mine, position, 0.0), axis=0, keepdims=True)
        allowed = (document == query_document) & (position <= query_position)
        bias[...] = jnp.where(allowed, 0.0, NEGATIVE)
        lane = lax.broadcasted_iota(jnp.int32, (ROWS, HEAD), 1)
        power = (lane % (HEAD // 2)).astype(F32) * (-2.0 / HEAD)
        angles = position * jnp.exp(power * math.log(ROPE_BASE))
        sine = jnp.sin(angles)
        turns[0] = jnp.cos(angles)
        turns[1] = jnp.where(lane < HEAD // 2, -sine, sine)

    def take_rows():
        await_recv(rows_in.at[pl.ds(0, SECTIONS - 1)], rows_recv)
        current[...] = rows_in[...].reshape(TILE, HEAD)

    def partner(j):
        return (z + jnp.where(j % 2 == 1, (j + 1) // 2, SECTIONS - j // 2)) % SECTIONS

    def send_packed(v, j):
        to = partner(j)
        remote(packed_all.at[v * SECTIONS + to], packed_in.at[v, z],
               packed_send.at[v], packed_recv.at[v], to, d).start()

    def send_pairs(v, j):
        to = partner(j)
        remote(pairs_all.at[v * SECTIONS + to], pairs_in.at[v, z],
               pair_send.at[v], pair_recv.at[v], to, d).start()

    def forward(layer):
        cosine, sine = turns[0], turns[1]
        cosine_all, sine_all = over_heads(cosine), over_heads(sine)
        x = current[...]
        saved[layer] = x
        gained = x * gain_rows(gains[layer % SECTIONS, layer // SECTIONS])
        pre = dot(side_by_side(gained).astype(BF16),
                  weight[layer].reshape(FEATURES, 2 * HEAD), 1, 0)
        scale = lax.rsqrt(row_mean(x * x) + EPSILON)
        saved_scale[layer] = scale
        pre = pre * scale
        normed = gained * over_heads(scale)
        queries = turn(normed, cosine_all, sine_all).astype(BF16)
        keys = turn(pre[:, :HEAD], cosine, sine).astype(BF16)
        values = pre[:, HEAD:].astype(BF16)
        scores = dot(keys, queries, 1, 1) * HEAD ** (-0.5) + bias[...]
        raised = jnp.exp(scores - jnp.max(scores, axis=0, keepdims=True))
        weights = raised / jnp.sum(raised, axis=0, keepdims=True)
        saved_queries[layer] = queries
        saved_keys[layer, 0] = keys
        saved_keys[layer, 1] = values
        saved_weights[layer] = weights
        wide = side_by_side(normed)
        packed_all[layer] = jnp.concatenate(
            [wide[:, :FEATURES // 2], wide[:, FEATURES // 2:]], axis=0).astype(BF16)
        current[...] = x + dot(weights.astype(BF16), values, 0, 0)

    def rows_at(layer, e, at, rows):
        if e == 0:
            return weight.at[layer, :, at, core, rows, :]
        return weight.at[layer, at, :, core, rows, :]

    def device_by(e, by):
        if e == 0:
            return (px * SIDE + (py + by) % SIDE) * 2 + core
        return (((px + by) % SIDE) * SIDE + py) * 2 + core

    def around(e, by):
        return ((py if e == 0 else px) + by) % SIDE

    every, low, high = pl.ds(0, PART), pl.ds(0, PART // 2), pl.ds(PART // 2, PART // 2)

    def stage_one(layer, e):
        line = rows_at(layer, e, around(e, 0), every)
        remote(line, line, ring_send.at[layer // SECTIONS, 0], ring_recv.at[layer, 0], z, device_by(e, 1)).start()
        remote(line, line, ring_send.at[layer // SECTIONS, 0], ring_recv.at[layer, 1], z, device_by(e, 3)).start()

    def stage_two(layer, e):
        left, right = around(e, 3), around(e, 1)
        await_recv(rows_at(layer, e, left, every), ring_recv.at[layer, 0])
        part = rows_at(layer, e, left, low)
        remote(part, part, ring_send.at[layer // SECTIONS, 1], ring_recv.at[layer, 2], z, device_by(e, 1)).start()
        await_recv(rows_at(layer, e, right, every), ring_recv.at[layer, 1])
        part = rows_at(layer, e, right, high)
        remote(part, part, ring_send.at[layer // SECTIONS, 1], ring_recv.at[layer, 3], z, device_by(e, 3)).start()

    def stage_three(layer, e):
        far = around(e, 2)
        await_recv(rows_at(layer, e, far, low), ring_recv.at[layer, 2])
        await_recv(rows_at(layer, e, far, high), ring_recv.at[layer, 3])
        half = weight.at[layer, :, :, core]
        remote(half, half, ring_send.at[layer // SECTIONS, 2], ring_recv.at[layer, 4], z, twin).start()

    def stage_four(layer, e):
        await_recv(weight.at[layer, :, :, 1 - core], ring_recv.at[layer, 4])

    def turn_of(t):
        @pl.when((t >= 1) & (t <= 8))
        def _():
            line_step(0, t)
            gain_step(t)

        @pl.when((t <= 7) & (t % 2 == 1))
        def _():
            line_step(1, t // 2)

        @pl.when((t >= 8) & (t <= 12))
        def _():
            line_step(1, t - 4)

        for late, stage in ((0, stage_one), (1, stage_two), (2, stage_three), (3, stage_four)):
            v = jnp.where(t - late <= 8, 0, 1)
            s = t - late - 8 * v

            @pl.when((s >= 1) & (s <= 8))
            def _():
                stage(v * SECTIONS + (z + SECTIONS - s) % SECTIONS, 0)

            @pl.when((s >= 1) & (s <= 7))
            def _():
                stage(v * SECTIONS + (z + s) % SECTIONS, 1)

        @pl.when(t == 3)
        def _():
            place_halves()

        @pl.when(t == 11)
        def _():
            take_rows()

        @pl.when((t >= 11) & (t <= 14))
        def _():
            loop(4 * (t - 11), 4 * (t - 11) + 4, forward)

        @pl.when(t == 14)
        def _():
            loop(1, SECTIONS, lambda j: send_packed(0, j))

    loop(1, 20, turn_of)

    loop(SECTIONS, LAYERS, forward)

    last_copy.wait()
    both = last[...].astype(F32)
    current[...] = stacked(jnp.where(z % 2 == 0, both[:ROWS], both[ROWS:]))

    def backward(step):
        layer = LAYERS - 1 - step
        cosine, sine = turns[0], turns[1]
        cosine_all, sine_all = over_heads(cosine), over_heads(sine)
        upstream = current[...]
        rounded = upstream.astype(BF16)
        keys = saved_keys[layer, 0]
        values = saved_keys[layer, 1]
        queries = saved_queries[layer]
        weights = saved_weights[layer]
        d_weights = dot(values, rounded, 1, 1)
        d_values = dot(weights.astype(BF16), rounded, 1, 0)
        inner = jnp.sum(d_weights * weights, axis=0, keepdims=True)
        d_scores = ((weights * HEAD ** (-0.5)) * (d_weights - inner)).astype(BF16)
        d_keys = dot(d_scores, queries, 1, 0)
        d_key_pre = unturn(d_keys, cosine, sine)
        pair = jnp.concatenate([d_key_pre, d_values], axis=1).astype(BF16)
        d_packed = stacked(dot(pair, weight[layer].reshape(FEATURES, 2 * HEAD), 1, 1))
        pairs_all[layer] = jnp.concatenate([d_key_pre, d_values], axis=0).astype(BF16)
        d_queries = dot(d_scores, keys, 0, 0)
        inside = jnp.sum((d_queries * queries.astype(F32)).reshape(HEADS, ROWS, HEAD), axis=0)
        inside = inside + d_keys * keys.astype(F32) + d_values * values.astype(F32)
        scale = saved_scale[layer]
        pull = jnp.sum(inside, axis=-1, keepdims=True) * (scale * scale * (1.0 / FEATURES))
        by = gain_rows(gains[layer % SECTIONS, layer // SECTIONS]) * over_heads(scale)
        known = upstream - saved[layer] * over_heads(pull)
        known = known + unturn(d_queries, cosine_all, sine_all) * by
        current[...] = known + d_packed * by

    def terms_of(v):
        others = pl.ds(0, SECTIONS - 1)
        await_recv(packed_in.at[v, others], packed_recv.at[v])
        await_recv(pairs_in.at[v, others], pair_recv.at[v])
        packed_in[v, z] = packed_all[v * SECTIONS + z]
        pairs_in[v, z] = pairs_all[v * SECTIONS + z]
        pair = pairs_in[v].astype(F32)
        pair = jnp.concatenate([pair[:, :ROWS], pair[:, ROWS:]], axis=2)
        nothing = jnp.zeros_like(pair)
        upper = jnp.concatenate([pair, nothing], axis=1).reshape(2 * TILE, 2 * HEAD)
        lower = jnp.concatenate([nothing, pair], axis=1).reshape(2 * TILE, 2 * HEAD)
        both = jnp.concatenate([upper, lower], axis=1).astype(BF16)
        product = dot(packed_in[v].reshape(2 * TILE, FEATURES // 2), both, 0, 0).astype(BF16)
        for g in range(GROUPS):
            rows = product[PART * (g % 16):PART * (g % 16 + 1)]
            terms[v, g // 2, g % 2] = rows[:, 2 * HEAD * (g // 16):2 * HEAD * (g // 16 + 1)]
        remote(terms.at[v, :, 1 - core], twin_in.at[v],
               twin_send.at[v], twin_recv.at[v], z, twin).start()

    def send_chips(v):
        await_recv(twin_in.at[v], twin_recv.at[v])
        chip_terms[v] = (terms[v, :, core].astype(F32) + twin_in[v].astype(F32)).astype(BF16)

        def send_chip(k):
            to = (chip + k) % (GROUPS // 2)
            remote(chip_terms.at[v, to], chip_in.at[v, chip],
                   chip_send.at[v], chip_recv.at[v], z, 2 * to + core).start()

        loop(1, GROUPS // 2, send_chip)
        chip_in[v, chip] = chip_terms[v, chip]

    def backward_step(j):
        backward(j)

        @pl.when((j >= 1) & (j < 8))
        def _():
            send_packed(1, 2 * j - 1)
            send_packed(1, 2 * j)

        @pl.when(j == 8)
        def _():
            send_packed(1, SECTIONS - 1)

        @pl.when((j >= SECTIONS) & (j < SECTIONS + 8))
        def _():
            send_pairs(1, 2 * (j - SECTIONS) + 1)

        @pl.when((j >= SECTIONS) & (j < SECTIONS + 7))
        def _():
            send_pairs(1, 2 * (j - SECTIONS) + 2)

        @pl.when(j == 27)
        def _():
            terms_of(1)

        @pl.when(j == 30)
        def _():
            send_chips(1)

    loop(0, LAYERS, backward_step)
    loop(1, SECTIONS, lambda j: send_pairs(0, j))

    back_out[...] = current[...].astype(BF16).astype(F32).reshape(SECTIONS, ROWS, HEAD)
    back_in[z] = back_out[z]

    def send_back(k):
        to = (z + k) % SECTIONS
        remote(back_out.at[to], back_in.at[z], back_send, back_recv, to, d).start()

    loop(1, SECTIONS, send_back)
    terms_of(0)

    await_recv(back_in.at[pl.ds(0, SECTIONS - 1)], back_recv)
    mine = back_in[...].reshape(TILE, HEAD).astype(BF16)
    home_out[...] = dot(placing[...], mine, 1, 0).reshape(GROUPS, ROWS, HEAD)
    home_in[d] = home_out[d]

    def send_home(k):
        to = (d + k) % GROUPS
        remote(home_out.at[to], home_in.at[d], home_send, home_recv, z, to).start()

    loop(1, GROUPS, send_home)
    send_chips(0)

    await_recv(home_in.at[pl.ds(0, GROUPS - 1)], home_recv)
    arrived = home_in[...].reshape(2 * TILE, HEAD).astype(BF16)
    grad_ref[...] = dot(sorting[...], arrived, 0, 0).astype(BF16)

    others = pl.ds(0, SECTIONS - 1)
    for v in range(2):
        await_send(weight.at[others, pl.ds(0, 2), :, 0], ring_send.at[v, 0])
        await_send(weight.at[others, 0, :, 0], ring_send.at[v, 1])
        await_send(weight.at[others, :, :, 0], ring_send.at[v, 2])
        await_send(weight.at[pl.ds(0, 8), 0, :, 0], zw_right.at[v])
        await_send(weight.at[pl.ds(0, 7), 0, :, 0], zw_left.at[v])
        await_send(packed_all.at[others], packed_send.at[v])
        await_send(pairs_all.at[others], pair_send.at[v])
    await_send(gains.at[pl.ds(0, 8)], zg_right)
    await_send(gains.at[pl.ds(0, 7)], zg_left)
    await_send(rows_out.at[others], rows_send)
    await_send(back_out.at[others], back_send)
    await_send(half_out.at[pl.ds(0, GROUPS - 1)], half_send)
    await_send(home_out.at[pl.ds(0, GROUPS - 1)], home_send)
    for v in range(2):
        await_send(twin_in.at[v], twin_send.at[v])

        await_recv(chip_in.at[v, others], chip_recv.at[v])
        await_send(chip_terms.at[v, others], chip_send.at[v])
        total = jnp.zeros((PART, 2 * HEAD), F32)
        for k in range(GROUPS // 2):
            total = total + chip_in[v, k].astype(F32)
        key_out_ref[v] = total[:, :HEAD]
        value_out_ref[v] = total[:, HEAD:]


def run_whole(hidden, lengths, route, gain, key_weight, value_weight, cotangent):
    whole = pl.BlockSpec(memory_space=pltpu.VMEM)
    remote = pl.BlockSpec(memory_space=pl.ANY)
    dma = pltpu.SemaphoreType.DMA
    small = pltpu.VMEM((SECTIONS, ROWS, HEAD), F32)
    large = pltpu.VMEM((GROUPS, ROWS, HEAD), F32)
    chips = GROUPS // 2
    return pl.pallas_call(
        whole_kernel,
        out_shape=(
            jax.ShapeDtypeStruct((TILE, HEAD), BF16),
            jax.ShapeDtypeStruct((2, PART, HEAD), F32),
            jax.ShapeDtypeStruct((2, PART, HEAD), F32),
        ),
        in_specs=[whole] * 4 + [remote] * 3,
        out_specs=(whole, whole, whole),
        scratch_shapes=[
            pltpu.VMEM((LAYERS, SIDE, SIDE, 2, PART, 2 * HEAD), BF16),
            pltpu.VMEM((SECTIONS, 2, HEADS, HEAD), F32),
            pltpu.VMEM((TILE, HEAD), F32),
            pltpu.VMEM((LAYERS, TILE, HEAD), F32),
            pltpu.VMEM((LAYERS, TILE, HEAD), BF16),
            pltpu.VMEM((LAYERS, 2, ROWS, HEAD), BF16),
            pltpu.VMEM((LAYERS, ROWS, TILE), F32),
            pltpu.VMEM((LAYERS, ROWS, 1), F32),
            pltpu.VMEM((ROWS, TILE), F32),
            pltpu.VMEM((2, ROWS, HEAD), F32),
            pltpu.VMEM((LAYERS, 2 * ROWS, FEATURES // 2), BF16),
            pltpu.VMEM((2, SECTIONS, 2 * ROWS, FEATURES // 2), BF16),
            pltpu.VMEM((LAYERS, 2 * ROWS, HEAD), BF16),
            pltpu.VMEM((2, SECTIONS, 2 * ROWS, HEAD), BF16),
            pltpu.VMEM((2, chips, 2, PART, 2 * HEAD), BF16),
            pltpu.VMEM((2, chips, PART, 2 * HEAD), BF16),
            pltpu.VMEM((2, chips, PART, 2 * HEAD), BF16),
            pltpu.VMEM((2, chips, PART, 2 * HEAD), BF16),
            pltpu.VMEM((2 * TILE, TILE), BF16),
            pltpu.VMEM((2 * TILE, TILE), BF16),
            large, large, small, small, small, small, large, large,
            pltpu.VMEM((2 * ROWS, FEATURES), BF16),
            dma(()), dma((2, 2)),
            dma((2, SECTIONS, SIDE)), dma((2,)), dma((2,)),
            dma((SECTIONS,)), dma(()), dma(()),
            dma((2, 3)), dma((LAYERS, 5)),
            dma((2,)), dma((2,)), dma((2,)), dma((2,)),
            dma(()), dma(()), dma(()), dma(()),
            dma(()), dma(()), dma(()), dma(()),
            dma((2,)), dma((2,)), dma((2,)), dma((2,)),
        ],
        compiler_params=pltpu.CompilerParams(
            collective_id=0, has_side_effects=True, vmem_limit_bytes=56 * 2**20),
    )(hidden, lengths, route, gain, key_weight, value_weight, cotangent)


def body(hidden, lengths, route, gain, key_weight, value_weight, cotangent):
    shares = (2, SIDE, SIDE, 2, PART, HEAD)
    return run_whole(
        hidden, lengths.T, route.T, gain,
        key_weight.reshape(shares), value_weight.reshape(shares), cotangent)


def solution(mesh):
    placed = (
        P("dp", "pipe"),
        P("dp", None),
        P("dp", None),
        P("pipe", None),
        P("pipe", None, None),
        P("pipe", None, None),
        P("dp", None),
    )
    return jax.shard_map(
        body,
        mesh=mesh,
        in_specs=placed,
        out_specs=(P("dp", "pipe"), P("pipe", "dp", None), P("pipe", "dp", None)),
        check_vma=False,
    )
```

```python
import math

import jax
import jax.numpy as jnp
from jax import lax
from jax.experimental import pallas as pl
from jax.experimental.pallas import tpu as pltpu
from jax.sharding import PartitionSpec as P

ROPE_BASE = 500000.0
EPSILON = 1e-05
NEGATIVE = -1e30
HEADS = 16
ROWS = 8
HEAD = 128
SECTIONS = 16
GROUPS = 32
LAYERS = 32
SIDE = 4
PART = 64
TILE = HEADS * ROWS
FEATURES = HEADS * HEAD
F32 = jnp.float32
BF16 = jnp.bfloat16
MESH = pl.DeviceIdType.MESH


def dot(a, b, over_a, over_b):
    return lax.dot_general(
        a, b, (((over_a,), (over_b,)), ((), ())), preferred_element_type=F32
    )


def swap_halves(flat):
    return pltpu.roll(flat, HEAD // 2, 1)


def turn(flat, cosine, sine):
    return flat * cosine + swap_halves(flat) * sine


def unturn(flat, cosine, sine):
    return flat * cosine - swap_halves(flat) * sine


def side_by_side(flat):
    return jnp.concatenate([flat[ROWS * h:ROWS * (h + 1)] for h in range(HEADS)], axis=1)


def stacked(wide):
    return jnp.concatenate([wide[:, HEAD * h:HEAD * (h + 1)] for h in range(HEADS)], axis=0)


def row_mean(flat):
    total = jnp.sum(flat.reshape(HEADS, ROWS, HEAD), axis=0)
    return jnp.sum(total, axis=-1, keepdims=True) * (1.0 / (HEADS * HEAD))


def over_heads(rows):
    return jnp.broadcast_to(rows[None], (HEADS, ROWS, rows.shape[-1])).reshape(
        HEADS * ROWS, rows.shape[-1]
    )


def gain_rows(gain):
    return jnp.broadcast_to(gain[:, None, :], (HEADS, ROWS, HEAD)).reshape(HEADS * ROWS, HEAD)


def whole_kernel(
    hidden_ref, lengths_ref, route_ref, gain_ref, key_ref, value_ref, cotangent_ref,
    grad_ref, key_out_ref, value_out_ref,
    weight, gains, current, saved, saved_queries, saved_keys, saved_weights, saved_scale, bias, turns,
    packed_all, packed_in, pairs_all, pairs_in, terms, twin_in, chip_terms, chip_in,
    sorting, placing, half_out, half_in, rows_out, rows_in, back_out, back_in, home_out, home_in,
    last, last_sem, own_sem, zw_recv, zw_right, zw_left, zg_recv, zg_right, zg_left,
    ring_send, ring_recv, packed_send, packed_recv, pair_send, pair_recv,
    half_send, half_recv, rows_send, rows_recv, back_send, back_recv, home_send, home_recv,
    twin_send, twin_recv, chip_send, chip_recv,
):
    z = lax.axis_index("pipe")
    d = lax.axis_index("dp")
    core = d % 2
    chip = d // 2
    px, py = chip // SIDE, chip % SIDE
    twin = chip * 2 + 1 - core
    z_next, z_before = (z + 1) % SECTIONS, (z + SECTIONS - 1) % SECTIONS

    def loop(low, high, run):
        lax.fori_loop(low, high, lambda i, c: (run(i), c)[1], 0)

    barrier = pltpu.get_barrier_semaphore()

    def greet_plane(k):
        pl.semaphore_signal(
            barrier, inc=1, device_id={"pipe": z, "dp": (d + k) % GROUPS}, device_id_type=MESH)

    def greet_line(k):
        pl.semaphore_signal(
            barrier, inc=1, device_id={"pipe": (z + k) % SECTIONS, "dp": d}, device_id_type=MESH)

    loop(1, GROUPS, greet_plane)
    loop(1, SECTIONS, greet_line)

    def remote(src, dst, send, recv, to_z, to_d):
        return pltpu.make_async_remote_copy(
            src_ref=src, dst_ref=dst, send_sem=send, recv_sem=recv,
            device_id={"pipe": to_z, "dp": to_d}, device_id_type=MESH,
        )

    def await_recv(ref, sem):
        remote(ref, ref, sem, sem, z, twin).wait_recv()

    def await_send(ref, sem):
        remote(ref, ref, sem, sem, z, twin).wait_send()

    owned = []
    for v in range(2):
        own = weight.at[v * SECTIONS + z]
        owned.append(pltpu.make_async_copy(
            key_ref.at[v], own.at[:, :, :, :, pl.ds(0, HEAD)], own_sem.at[v, 0]))
        owned.append(pltpu.make_async_copy(
            value_ref.at[v], own.at[:, :, :, :, pl.ds(HEAD, HEAD)], own_sem.at[v, 1]))
    for copy in owned:
        copy.start()
    upstream_rows = pl.ds(pl.multiple_of(z // 2 * 2 * ROWS, 2 * ROWS), 2 * ROWS)
    last_copy = pltpu.make_async_copy(cotangent_ref.at[upstream_rows, :], last, last_sem)
    last_copy.start()
    for v in range(2):
        gains[z, v] = jnp.concatenate(
            [gain_ref[v:v + 1, HEAD * h:HEAD * (h + 1)] for h in range(HEADS)], axis=0)

    row = lax.broadcasted_iota(jnp.int32, (2 * TILE, 2 * TILE), 0)
    col = lax.broadcasted_iota(jnp.int32, (2 * TILE, 2 * TILE), 1)
    kind_row = (col // TILE) * (ROWS // 2) + col % (ROWS // 2)
    micro = lax.broadcasted_iota(jnp.int32, (SECTIONS, 2 * TILE), 0)
    lane = lax.broadcasted_iota(jnp.int32, (SECTIONS, 2 * TILE), 1) % TILE
    spread_out = jnp.where(micro == lane // ROWS, 1.0, 0.0).astype(BF16)
    lane_route = dot(route_ref[...].astype(F32).astype(BF16), spread_out, 1, 0)
    leading = lane[0:1] // (ROWS // 2) % 2 == 0
    lane_route = jnp.where(leading, lane_route[0:1], lane_route[1:2])
    chosen = (lane_route == (row // ROWS).astype(F32)) & (row % ROWS == kind_row)
    sort = jnp.where(chosen, 1.0, 0.0).astype(BF16)
    sorting[...] = sort[:, :TILE]
    row = lax.broadcasted_iota(jnp.int32, (TILE, SECTIONS), 0)
    col = lax.broadcasted_iota(jnp.int32, (TILE, SECTIONS), 1)
    spread_out = jnp.where(row // ROWS == col, 1.0, 0.0).astype(BF16)
    row_lengths = dot(spread_out, lengths_ref[...].astype(F32).astype(BF16), 1, 1)
    row = lax.broadcasted_iota(jnp.int32, (TILE, HEAD), 0)
    lane = lax.broadcasted_iota(jnp.int32, (TILE, HEAD), 1)
    at = (row % ROWS).astype(F32)
    ends = [jnp.broadcast_to(row_lengths[:, 0:1], (TILE, HEAD))]
    for k in range(1, row_lengths.shape[1] - 1):
        ends.append(ends[-1] + row_lengths[:, k:k + 1])
    document = jnp.zeros((TILE, HEAD), F32)
    opening = jnp.zeros((TILE, HEAD), F32)
    for end in ends:
        document = document + jnp.where(at >= end, 1.0, 0.0)
        opening = jnp.where(at >= end, end, opening)
    slots = (row // (ROWS // 2)).astype(F32)
    tags = jnp.where(lane < HEAD // 4, document, jnp.where(lane < HEAD // 2, at - opening, slots))
    source = jnp.concatenate([hidden_ref[...], tags.astype(BF16)], axis=0)
    half_out[...] = dot(sort, source, 1, 0).reshape(GROUPS, ROWS, HEAD)
    half_in[d] = half_out[d]

    pl.semaphore_wait(barrier, GROUPS + SECTIONS - 2)

    def send_half(k):
        to = (d + k) % GROUPS
        remote(half_out.at[to], half_in.at[d], half_send, half_recv, z, to).start()

    for copy in owned[:2]:
        copy.wait()

    def row_of(layer, e):
        return weight.at[layer, :, py, core] if e == 0 else weight.at[layer, px, :, core]

    def line_step(v, s):
        on_left = (z + SECTIONS - s) % SECTIONS
        on_right = (z + s) % SECTIONS
        for q in range(2):
            two = pl.ds(2 * q, 2)
            left = weight.at[v * SECTIONS + on_left, two, py, core]
            right = weight.at[v * SECTIONS + on_right, px, two, core]
            left_sem = zw_recv.at[v, on_left, q]
            right_sem = zw_recv.at[v, on_right, q]

            @pl.when(s >= 1)
            def _():
                await_recv(left, left_sem)

            @pl.when(s <= 7)
            def _():
                remote(left, left, zw_right.at[v], left_sem, z_next, d).start()

            @pl.when((s >= 1) & (s <= 7))
            def _():
                await_recv(right, right_sem)

            @pl.when(s <= 6)
            def _():
                remote(right, right, zw_left.at[v], right_sem, z_before, d).start()

    def gain_step(s):
        on_left = (z + SECTIONS - s) % SECTIONS
        on_right = (z + s) % SECTIONS

        @pl.when(s >= 1)
        def _():
            await_recv(gains.at[on_left], zg_recv.at[on_left])

        @pl.when(s <= 7)
        def _():
            line = gains.at[on_left]
            remote(line, line, zg_right, zg_recv.at[on_left], z_next, d).start()

        @pl.when((s >= 1) & (s <= 7))
        def _():
            await_recv(gains.at[on_right], zg_recv.at[on_right])

        @pl.when(s <= 6)
        def _():
            line = gains.at[on_right]
            remote(line, line, zg_left, zg_recv.at[on_right], z_before, d).start()

    line_step(0, 0)
    gain_step(0)
    loop(1, GROUPS, send_half)
    for copy in owned[2:]:
        copy.wait()

    def send_rows(k):
        to = (z + k) % SECTIONS
        remote(rows_out.at[to], rows_in.at[z], rows_send, rows_recv, to, d).start()

    def place_halves():
        await_recv(half_in.at[pl.ds(0, GROUPS - 1)], half_recv)
        arrived = half_in[...]
        slot = jnp.broadcast_to(arrived[:, 4:5, HEAD // 2:HEAD // 2 + 1], (GROUPS, ROWS, 1))
        slot = slot.reshape(2 * TILE, 1)
        arrived = arrived.reshape(2 * TILE, HEAD).astype(BF16)
        row = lax.broadcasted_iota(jnp.int32, (2 * TILE, TILE), 0) % ROWS
        col = lax.broadcasted_iota(jnp.int32, (2 * TILE, TILE), 1)
        same = slot == (col // (ROWS // 2)).astype(F32)
        place = jnp.where(same & (row == col % (ROWS // 2)), 1.0, 0.0).astype(BF16)
        place_tags = jnp.where(same & (row == col % (ROWS // 2) + ROWS // 2), 1.0, 0.0).astype(BF16)
        placing[...] = place
        rows_out[...] = dot(place, arrived, 0, 0).reshape(SECTIONS, ROWS, HEAD)
        home_out[pl.ds(0, SECTIONS)] = dot(place_tags, arrived, 0, 0).reshape(SECTIONS, ROWS, HEAD)
        rows_in[z] = rows_out[z]

        loop(1, SECTIONS, send_rows)

        tags = home_out[z]
        document = jnp.broadcast_to(tags[:, 0:1], (ROWS, TILE))
        position = jnp.broadcast_to(tags[:, HEAD // 4:HEAD // 4 + 1], (ROWS, TILE))
        lane = lax.broadcasted_iota(jnp.int32, (ROWS, TILE), 1) % ROWS
        mine = lane == lax.broadcasted_iota(jnp.int32, (ROWS, TILE), 0)
        query_document = jnp.sum(jnp.where(mine, document, 0.0), axis=0, keepdims=True)
        query_position = jnp.sum(jnp.where(mine, position, 0.0), axis=0, keepdims=True)
        allowed = (document == query_document) & (position <= query_position)
        bias[...] = jnp.where(allowed, 0.0, NEGATIVE)
        lane = lax.broadcasted_iota(jnp.int32, (ROWS, HEAD), 1)
        power = (lane % (HEAD // 2)).astype(F32) * (-2.0 / HEAD)
        angles = position * jnp.exp(power * math.log(ROPE_BASE))
        sine = jnp.sin(angles)
        turns[0] = jnp.cos(angles)
        turns[1] = jnp.where(lane < HEAD // 2, -sine, sine)

    def take_rows():
        await_recv(rows_in.at[pl.ds(0, SECTIONS - 1)], rows_recv)
        current[...] = rows_in[...].reshape(TILE, HEAD)

    def partner(j):
        return (z + jnp.where(j % 2 == 1, (j + 1) // 2, SECTIONS - j // 2)) % SECTIONS

    def send_packed(v, j):
        to = partner(j)
        remote(packed_all.at[v * SECTIONS + to], packed_in.at[v, z],
               packed_send.at[v], packed_recv.at[v], to, d).start()

    def send_pairs(v, j):
        to = partner(j)
        remote(pairs_all.at[v * SECTIONS + to], pairs_in.at[v, z],
               pair_send.at[v], pair_recv.at[v], to, d).start()

    def forward(layer):
        cosine, sine = turns[0], turns[1]
        cosine_all, sine_all = over_heads(cosine), over_heads(sine)
        x = current[...]
        saved[layer] = x
        gained = x * gain_rows(gains[layer % SECTIONS, layer // SECTIONS])
        pre = dot(side_by_side(gained).astype(BF16),
                  weight[layer].reshape(FEATURES, 2 * HEAD), 1, 0)
        scale = lax.rsqrt(row_mean(x * x) + EPSILON)
        saved_scale[layer] = scale
        pre = pre * scale
        normed = gained * over_heads(scale)
        queries = turn(normed, cosine_all, sine_all).astype(BF16)
        keys = turn(pre[:, :HEAD], cosine, sine).astype(BF16)
        values = pre[:, HEAD:].astype(BF16)
        scores = dot(keys, queries, 1, 1) * HEAD ** (-0.5) + bias[...]
        raised = jnp.exp(scores - jnp.max(scores, axis=0, keepdims=True))
        weights = raised / jnp.sum(raised, axis=0, keepdims=True)
        saved_queries[layer] = queries
        saved_keys[layer, 0] = keys
        saved_keys[layer, 1] = values
        saved_weights[layer] = weights
        wide = side_by_side(normed)
        packed_all[layer] = jnp.concatenate(
            [wide[:, :FEATURES // 2], wide[:, FEATURES // 2:]], axis=0).astype(BF16)
        current[...] = x + dot(weights.astype(BF16), values, 0, 0)

    def rows_at(layer, e, at, rows):
        if e == 0:
            return weight.at[layer, :, at, core, rows, :]
        return weight.at[layer, at, :, core, rows, :]

    def device_by(e, by):
        if e == 0:
            return (px * SIDE + (py + by) % SIDE) * 2 + core
        return (((px + by) % SIDE) * SIDE + py) * 2 + core

    def around(e, by):
        return ((py if e == 0 else px) + by) % SIDE

    every, low, high = pl.ds(0, PART), pl.ds(0, PART // 2), pl.ds(PART // 2, PART // 2)

    def stage_one(layer, e):
        line = rows_at(layer, e, around(e, 0), every)
        remote(line, line, ring_send.at[layer // SECTIONS, 0], ring_recv.at[layer, 0], z, device_by(e, 1)).start()
        remote(line, line, ring_send.at[layer // SECTIONS, 0], ring_recv.at[layer, 1], z, device_by(e, 3)).start()

    def stage_two(layer, e):
        left, right = around(e, 3), around(e, 1)
        await_recv(rows_at(layer, e, left, every), ring_recv.at[layer, 0])
        part = rows_at(layer, e, left, low)
        remote(part, part, ring_send.at[layer // SECTIONS, 1], ring_recv.at[layer, 2], z, device_by(e, 1)).start()
        await_recv(rows_at(layer, e, right, every), ring_recv.at[layer, 1])
        part = rows_at(layer, e, right, high)
        remote(part, part, ring_send.at[layer // SECTIONS, 1], ring_recv.at[layer, 3], z, device_by(e, 3)).start()

    def stage_three(layer, e):
        far = around(e, 2)
        await_recv(rows_at(layer, e, far, low), ring_recv.at[layer, 2])
        await_recv(rows_at(layer, e, far, high), ring_recv.at[layer, 3])
        half = weight.at[layer, :, :, core]
        remote(half, half, ring_send.at[layer // SECTIONS, 2], ring_recv.at[layer, 4], z, twin).start()

    def stage_four(layer, e):
        await_recv(weight.at[layer, :, :, 1 - core], ring_recv.at[layer, 4])

    def turn_of(t):
        @pl.when((t >= 1) & (t <= 8))
        def _():
            line_step(0, t)
            gain_step(t)

        @pl.when((t <= 7) & (t % 2 == 1))
        def _():
            line_step(1, t // 2)

        @pl.when((t >= 8) & (t <= 12))
        def _():
            line_step(1, t - 4)

        for late, stage in ((0, stage_one), (1, stage_two), (2, stage_three), (3, stage_four)):
            v = jnp.where(t - late <= 8, 0, 1)
            s = t - late - 8 * v

            @pl.when((s >= 1) & (s <= 8))
            def _():
                stage(v * SECTIONS + (z + SECTIONS - s) % SECTIONS, 0)

            @pl.when((s >= 1) & (s <= 7))
            def _():
                stage(v * SECTIONS + (z + s) % SECTIONS, 1)

        @pl.when(t == 9)
        def _():
            place_halves()

        @pl.when(t == 11)
        def _():
            take_rows()

        @pl.when((t >= 11) & (t <= 14))
        def _():
            loop(4 * (t - 11), 4 * (t - 11) + 4, forward)

        @pl.when(t == 14)
        def _():
            loop(1, SECTIONS, lambda j: send_packed(0, j))

    loop(1, 20, turn_of)

    loop(SECTIONS, LAYERS, forward)

    last_copy.wait()
    both = last[...].astype(F32)
    current[...] = stacked(jnp.where(z % 2 == 0, both[:ROWS], both[ROWS:]))

    def backward(step):
        layer = LAYERS - 1 - step
        cosine, sine = turns[0], turns[1]
        cosine_all, sine_all = over_heads(cosine), over_heads(sine)
        upstream = current[...]
        rounded = upstream.astype(BF16)
        keys = saved_keys[layer, 0]
        values = saved_keys[layer, 1]
        queries = saved_queries[layer]
        weights = saved_weights[layer]
        d_weights = dot(values, rounded, 1, 1)
        d_values = dot(weights.astype(BF16), rounded, 1, 0)
        inner = jnp.sum(d_weights * weights, axis=0, keepdims=True)
        d_scores = ((weights * HEAD ** (-0.5)) * (d_weights - inner)).astype(BF16)
        d_keys = dot(d_scores, queries, 1, 0)
        d_key_pre = unturn(d_keys, cosine, sine)
        pair = jnp.concatenate([d_key_pre, d_values], axis=1).astype(BF16)
        d_packed = stacked(dot(pair, weight[layer].reshape(FEATURES, 2 * HEAD), 1, 1))
        pairs_all[layer] = jnp.concatenate([d_key_pre, d_values], axis=0).astype(BF16)
        d_queries = dot(d_scores, keys, 0, 0)
        inside = jnp.sum((d_queries * queries.astype(F32)).reshape(HEADS, ROWS, HEAD), axis=0)
        inside = inside + d_keys * keys.astype(F32) + d_values * values.astype(F32)
        scale = saved_scale[layer]
        pull = jnp.sum(inside, axis=-1, keepdims=True) * (scale * scale * (1.0 / FEATURES))
        by = gain_rows(gains[layer % SECTIONS, layer // SECTIONS]) * over_heads(scale)
        known = upstream - saved[layer] * over_heads(pull)
        known = known + unturn(d_queries, cosine_all, sine_all) * by
        current[...] = known + d_packed * by

    def terms_of(v):
        others = pl.ds(0, SECTIONS - 1)
        await_recv(packed_in.at[v, others], packed_recv.at[v])
        await_recv(pairs_in.at[v, others], pair_recv.at[v])
        packed_in[v, z] = packed_all[v * SECTIONS + z]
        pairs_in[v, z] = pairs_all[v * SECTIONS + z]
        pair = pairs_in[v].astype(F32)
        pair = jnp.concatenate([pair[:, :ROWS], pair[:, ROWS:]], axis=2)
        nothing = jnp.zeros_like(pair)
        upper = jnp.concatenate([pair, nothing], axis=1).reshape(2 * TILE, 2 * HEAD)
        lower = jnp.concatenate([nothing, pair], axis=1).reshape(2 * TILE, 2 * HEAD)
        both = jnp.concatenate([upper, lower], axis=1).astype(BF16)
        product = dot(packed_in[v].reshape(2 * TILE, FEATURES // 2), both, 0, 0).astype(BF16)
        for g in range(GROUPS):
            rows = product[PART * (g % 16):PART * (g % 16 + 1)]
            terms[v, g // 2, g % 2] = rows[:, 2 * HEAD * (g // 16):2 * HEAD * (g // 16 + 1)]
        remote(terms.at[v, :, 1 - core], twin_in.at[v],
               twin_send.at[v], twin_recv.at[v], z, twin).start()

    def send_chips(v):
        await_recv(twin_in.at[v], twin_recv.at[v])
        chip_terms[v] = (terms[v, :, core].astype(F32) + twin_in[v].astype(F32)).astype(BF16)

        def send_chip(k):
            to = (chip + k) % (GROUPS // 2)
            remote(chip_terms.at[v, to], chip_in.at[v, chip],
                   chip_send.at[v], chip_recv.at[v], z, 2 * to + core).start()

        loop(1, GROUPS // 2, send_chip)
        chip_in[v, chip] = chip_terms[v, chip]

    def backward_step(j):
        backward(j)

        @pl.when((j >= 1) & (j < 8))
        def _():
            send_packed(1, 2 * j - 1)
            send_packed(1, 2 * j)

        @pl.when(j == 8)
        def _():
            send_packed(1, SECTIONS - 1)

        @pl.when((j >= SECTIONS) & (j < SECTIONS + 8))
        def _():
            send_pairs(1, 2 * (j - SECTIONS) + 1)

        @pl.when((j >= SECTIONS) & (j < SECTIONS + 7))
        def _():
            send_pairs(1, 2 * (j - SECTIONS) + 2)

        layer = LAYERS - 1 - j

        @pl.when((j >= SECTIONS) & (layer != z))
        def _():
            remote(pairs_all.at[layer], pairs_in.at[0, z],
                   pair_send.at[0], pair_recv.at[0], layer, d).start()

    loop(0, LAYERS, backward_step)

    back_out[...] = current[...].astype(BF16).astype(F32).reshape(SECTIONS, ROWS, HEAD)
    back_in[z] = back_out[z]

    def send_back(k):
        to = (z + k) % SECTIONS
        remote(back_out.at[to], back_in.at[z], back_send, back_recv, to, d).start()

    loop(1, SECTIONS, send_back)
    terms_of(1)
    terms_of(0)

    await_recv(back_in.at[pl.ds(0, SECTIONS - 1)], back_recv)
    mine = back_in[...].reshape(TILE, HEAD).astype(BF16)
    home_out[...] = dot(placing[...], mine, 1, 0).reshape(GROUPS, ROWS, HEAD)
    home_in[d] = home_out[d]

    def send_home(k):
        to = (d + k) % GROUPS
        remote(home_out.at[to], home_in.at[d], home_send, home_recv, z, to).start()

    loop(1, GROUPS, send_home)
    send_chips(1)
    send_chips(0)

    await_recv(home_in.at[pl.ds(0, GROUPS - 1)], home_recv)
    arrived = home_in[...].reshape(2 * TILE, HEAD).astype(BF16)
    grad_ref[...] = dot(sorting[...], arrived, 0, 0).astype(BF16)

    others = pl.ds(0, SECTIONS - 1)
    for v in range(2):
        await_send(weight.at[others, pl.ds(0, 2), :, 0], ring_send.at[v, 0])
        await_send(weight.at[others, 0, :, 0], ring_send.at[v, 1])
        await_send(weight.at[others, :, :, 0], ring_send.at[v, 2])
        await_send(weight.at[pl.ds(0, 8), 0, :, 0], zw_right.at[v])
        await_send(weight.at[pl.ds(0, 7), 0, :, 0], zw_left.at[v])
        await_send(packed_all.at[others], packed_send.at[v])
        await_send(pairs_all.at[others], pair_send.at[v])
    await_send(gains.at[pl.ds(0, 8)], zg_right)
    await_send(gains.at[pl.ds(0, 7)], zg_left)
    await_send(rows_out.at[others], rows_send)
    await_send(back_out.at[others], back_send)
    await_send(half_out.at[pl.ds(0, GROUPS - 1)], half_send)
    await_send(home_out.at[pl.ds(0, GROUPS - 1)], home_send)
    for v in range(2):
        await_send(twin_in.at[v], twin_send.at[v])

        await_recv(chip_in.at[v, others], chip_recv.at[v])
        await_send(chip_terms.at[v, others], chip_send.at[v])
        total = jnp.zeros((PART, 2 * HEAD), F32)
        for k in range(GROUPS // 2):
            total = total + chip_in[v, k].astype(F32)
        key_out_ref[v] = total[:, :HEAD]
        value_out_ref[v] = total[:, HEAD:]


def run_whole(hidden, lengths, route, gain, key_weight, value_weight, cotangent):
    whole = pl.BlockSpec(memory_space=pltpu.VMEM)
    remote = pl.BlockSpec(memory_space=pl.ANY)
    dma = pltpu.SemaphoreType.DMA
    small = pltpu.VMEM((SECTIONS, ROWS, HEAD), F32)
    large = pltpu.VMEM((GROUPS, ROWS, HEAD), F32)
    chips = GROUPS // 2
    return pl.pallas_call(
        whole_kernel,
        out_shape=(
            jax.ShapeDtypeStruct((TILE, HEAD), BF16),
            jax.ShapeDtypeStruct((2, PART, HEAD), F32),
            jax.ShapeDtypeStruct((2, PART, HEAD), F32),
        ),
        in_specs=[whole] * 4 + [remote] * 3,
        out_specs=(whole, whole, whole),
        scratch_shapes=[
            pltpu.VMEM((LAYERS, SIDE, SIDE, 2, PART, 2 * HEAD), BF16),
            pltpu.VMEM((SECTIONS, 2, HEADS, HEAD), F32),
            pltpu.VMEM((TILE, HEAD), F32),
            pltpu.VMEM((LAYERS, TILE, HEAD), F32),
            pltpu.VMEM((LAYERS, TILE, HEAD), BF16),
            pltpu.VMEM((LAYERS, 2, ROWS, HEAD), BF16),
            pltpu.VMEM((LAYERS, ROWS, TILE), F32),
            pltpu.VMEM((LAYERS, ROWS, 1), F32),
            pltpu.VMEM((ROWS, TILE), F32),
            pltpu.VMEM((2, ROWS, HEAD), F32),
            pltpu.VMEM((LAYERS, 2 * ROWS, FEATURES // 2), BF16),
            pltpu.VMEM((2, SECTIONS, 2 * ROWS, FEATURES // 2), BF16),
            pltpu.VMEM((LAYERS, 2 * ROWS, HEAD), BF16),
            pltpu.VMEM((2, SECTIONS, 2 * ROWS, HEAD), BF16),
            pltpu.VMEM((2, chips, 2, PART, 2 * HEAD), BF16),
            pltpu.VMEM((2, chips, PART, 2 * HEAD), BF16),
            pltpu.VMEM((2, chips, PART, 2 * HEAD), BF16),
            pltpu.VMEM((2, chips, PART, 2 * HEAD), BF16),
            pltpu.VMEM((2 * TILE, TILE), BF16),
            pltpu.VMEM((2 * TILE, TILE), BF16),
            large, large, small, small, small, small, large, large,
            pltpu.VMEM((2 * ROWS, FEATURES), BF16),
            dma(()), dma((2, 2)),
            dma((2, SECTIONS, 2)), dma((2,)), dma((2,)),
            dma((SECTIONS,)), dma(()), dma(()),
            dma((2, 3)), dma((LAYERS, 5)),
            dma((2,)), dma((2,)), dma((2,)), dma((2,)),
            dma(()), dma(()), dma(()), dma(()),
            dma(()), dma(()), dma(()), dma(()),
            dma((2,)), dma((2,)), dma((2,)), dma((2,)),
        ],
        compiler_params=pltpu.CompilerParams(
            collective_id=0, has_side_effects=True, vmem_limit_bytes=56 * 2**20),
    )(hidden, lengths, route, gain, key_weight, value_weight, cotangent)


def body(hidden, lengths, route, gain, key_weight, value_weight, cotangent):
    shares = (2, SIDE, SIDE, 2, PART, HEAD)
    return run_whole(
        hidden, lengths.T, route.T, gain,
        key_weight.reshape(shares), value_weight.reshape(shares), cotangent)


def solution(mesh):
    placed = (
        P("dp", "pipe"),
        P("dp", None),
        P("dp", None),
        P("pipe", None),
        P("pipe", None, None),
        P("pipe", None, None),
        P("dp", None),
    )
    return jax.shard_map(
        body,
        mesh=mesh,
        in_specs=placed,
        out_specs=(P("dp", "pipe"), P("pipe", "dp", None), P("pipe", "dp", None)),
        check_vma=False,
    )
```

```python
import math

import jax
import jax.numpy as jnp
from jax import lax
from jax.experimental import pallas as pl
from jax.experimental.pallas import tpu as pltpu
from jax.sharding import PartitionSpec as P

ROPE_BASE = 500000.0
EPSILON = 1e-05
NEGATIVE = -1e30
HEADS = 16
ROWS = 8
HEAD = 128
SECTIONS = 16
GROUPS = 32
LAYERS = 32
SIDE = 4
PART = 64
TILE = HEADS * ROWS
FEATURES = HEADS * HEAD
F32 = jnp.float32
BF16 = jnp.bfloat16
MESH = pl.DeviceIdType.MESH


def dot(a, b, over_a, over_b):
    return lax.dot_general(
        a, b, (((over_a,), (over_b,)), ((), ())), preferred_element_type=F32
    )


def swap_halves(flat):
    return pltpu.roll(flat, HEAD // 2, 1)


def turn(flat, cosine, sine):
    return flat * cosine + swap_halves(flat) * sine


def unturn(flat, cosine, sine):
    return flat * cosine - swap_halves(flat) * sine


def side_by_side(flat):
    return jnp.concatenate([flat[ROWS * h:ROWS * (h + 1)] for h in range(HEADS)], axis=1)


def stacked(wide):
    return jnp.concatenate([wide[:, HEAD * h:HEAD * (h + 1)] for h in range(HEADS)], axis=0)


def row_mean(flat):
    total = jnp.sum(flat.reshape(HEADS, ROWS, HEAD), axis=0)
    return jnp.sum(total, axis=-1, keepdims=True) * (1.0 / (HEADS * HEAD))


def over_heads(rows):
    return jnp.broadcast_to(rows[None], (HEADS, ROWS, rows.shape[-1])).reshape(
        HEADS * ROWS, rows.shape[-1]
    )


def gain_rows(gain):
    return jnp.broadcast_to(gain[:, None, :], (HEADS, ROWS, HEAD)).reshape(HEADS * ROWS, HEAD)


def whole_kernel(
    hidden_ref, lengths_ref, route_ref, gain_ref, key_ref, value_ref, cotangent_ref,
    grad_ref, key_out_ref, value_out_ref,
    weight, gains, current, saved, saved_queries, saved_keys, saved_weights, saved_scale, bias, turns,
    packed_all, packed_in, pairs_all, pairs_in, terms, twin_in, chip_terms, chip_in,
    sorting, placing, half_out, half_in, rows_out, rows_in, back_out, back_in, home_out, home_in,
    last, last_sem, own_sem, zw_recv, zw_right, zw_left, zg_recv, zg_right, zg_left,
    ring_send, ring_recv, packed_send, packed_recv, pair_send, pair_recv,
    half_send, half_recv, rows_send, rows_recv, back_send, back_recv, home_send, home_recv,
    twin_send, twin_recv, chip_send, chip_recv,
):
    z = lax.axis_index("pipe")
    d = lax.axis_index("dp")
    core = d % 2
    chip = d // 2
    px, py = chip // SIDE, chip % SIDE
    twin = chip * 2 + 1 - core
    z_next, z_before = (z + 1) % SECTIONS, (z + SECTIONS - 1) % SECTIONS

    def loop(low, high, run):
        lax.fori_loop(low, high, lambda i, c: (run(i), c)[1], 0)

    barrier = pltpu.get_barrier_semaphore()

    def greet_plane(k):
        pl.semaphore_signal(
            barrier, inc=1, device_id={"pipe": z, "dp": (d + k) % GROUPS}, device_id_type=MESH)

    def greet_line(k):
        pl.semaphore_signal(
            barrier, inc=1, device_id={"pipe": (z + k) % SECTIONS, "dp": d}, device_id_type=MESH)

    loop(1, GROUPS, greet_plane)
    loop(1, SECTIONS, greet_line)

    def remote(src, dst, send, recv, to_z, to_d):
        return pltpu.make_async_remote_copy(
            src_ref=src, dst_ref=dst, send_sem=send, recv_sem=recv,
            device_id={"pipe": to_z, "dp": to_d}, device_id_type=MESH,
        )

    def await_recv(ref, sem):
        remote(ref, ref, sem, sem, z, twin).wait_recv()

    def await_send(ref, sem):
        remote(ref, ref, sem, sem, z, twin).wait_send()

    owned = []
    for v in range(2):
        own = weight.at[v * SECTIONS + z]
        owned.append(pltpu.make_async_copy(
            key_ref.at[v], own.at[:, :, :, :, pl.ds(0, HEAD)], own_sem.at[v, 0]))
        owned.append(pltpu.make_async_copy(
            value_ref.at[v], own.at[:, :, :, :, pl.ds(HEAD, HEAD)], own_sem.at[v, 1]))
    for copy in owned:
        copy.start()
    upstream_rows = pl.ds(pl.multiple_of(z // 2 * 2 * ROWS, 2 * ROWS), 2 * ROWS)
    last_copy = pltpu.make_async_copy(cotangent_ref.at[upstream_rows, :], last, last_sem)
    last_copy.start()
    for v in range(2):
        gains[z, v] = jnp.concatenate(
            [gain_ref[v:v + 1, HEAD * h:HEAD * (h + 1)] for h in range(HEADS)], axis=0)

    row = lax.broadcasted_iota(jnp.int32, (2 * TILE, 2 * TILE), 0)
    col = lax.broadcasted_iota(jnp.int32, (2 * TILE, 2 * TILE), 1)
    kind_row = (col // TILE) * (ROWS // 2) + col % (ROWS // 2)
    micro = lax.broadcasted_iota(jnp.int32, (SECTIONS, 2 * TILE), 0)
    lane = lax.broadcasted_iota(jnp.int32, (SECTIONS, 2 * TILE), 1) % TILE
    spread_out = jnp.where(micro == lane // ROWS, 1.0, 0.0).astype(BF16)
    lane_route = dot(route_ref[...].astype(F32).astype(BF16), spread_out, 1, 0)
    leading = lane[0:1] // (ROWS // 2) % 2 == 0
    lane_route = jnp.where(leading, lane_route[0:1], lane_route[1:2])
    chosen = (lane_route == (row // ROWS).astype(F32)) & (row % ROWS == kind_row)
    sort = jnp.where(chosen, 1.0, 0.0).astype(BF16)
    sorting[...] = sort[:, :TILE]
    row = lax.broadcasted_iota(jnp.int32, (TILE, SECTIONS), 0)
    col = lax.broadcasted_iota(jnp.int32, (TILE, SECTIONS), 1)
    spread_out = jnp.where(row // ROWS == col, 1.0, 0.0).astype(BF16)
    row_lengths = dot(spread_out, lengths_ref[...].astype(F32).astype(BF16), 1, 1)
    row = lax.broadcasted_iota(jnp.int32, (TILE, HEAD), 0)
    lane = lax.broadcasted_iota(jnp.int32, (TILE, HEAD), 1)
    at = (row % ROWS).astype(F32)
    ends = [jnp.broadcast_to(row_lengths[:, 0:1], (TILE, HEAD))]
    for k in range(1, row_lengths.shape[1] - 1):
        ends.append(ends[-1] + row_lengths[:, k:k + 1])
    document = jnp.zeros((TILE, HEAD), F32)
    opening = jnp.zeros((TILE, HEAD), F32)
    for end in ends:
        document = document + jnp.where(at >= end, 1.0, 0.0)
        opening = jnp.where(at >= end, end, opening)
    slots = (row // (ROWS // 2)).astype(F32)
    tags = jnp.where(lane < HEAD // 4, document, jnp.where(lane < HEAD // 2, at - opening, slots))
    source = jnp.concatenate([hidden_ref[...], tags.astype(BF16)], axis=0)
    half_out[...] = dot(sort, source, 1, 0).reshape(GROUPS, ROWS, HEAD)
    half_in[d] = half_out[d]

    pl.semaphore_wait(barrier, GROUPS + SECTIONS - 2)

    def send_half(k):
        to = (d + k) % GROUPS
        remote(half_out.at[to], half_in.at[d], half_send, half_recv, z, to).start()

    for copy in owned[:2]:
        copy.wait()

    def row_of(layer, e):
        return weight.at[layer, :, py, core] if e == 0 else weight.at[layer, px, :, core]

    def line_step(v, s):
        on_left = (z + SECTIONS - s) % SECTIONS
        on_right = (z + s) % SECTIONS
        for q in range(2):
            two = pl.ds(2 * q, 2)
            left = weight.at[v * SECTIONS + on_left, two, py, core]
            right = weight.at[v * SECTIONS + on_right, px, two, core]
            left_sem = zw_recv.at[v, on_left, q]
            right_sem = zw_recv.at[v, on_right, q]

            @pl.when(s >= 1)
            def _():
                await_recv(left, left_sem)

            @pl.when(s <= 7)
            def _():
                remote(left, left, zw_right.at[v], left_sem, z_next, d).start()

            @pl.when((s >= 1) & (s <= 7))
            def _():
                await_recv(right, right_sem)

            @pl.when(s <= 6)
            def _():
                remote(right, right, zw_left.at[v], right_sem, z_before, d).start()

    def gain_step(s):
        on_left = (z + SECTIONS - s) % SECTIONS
        on_right = (z + s) % SECTIONS

        @pl.when(s >= 1)
        def _():
            await_recv(gains.at[on_left], zg_recv.at[on_left])

        @pl.when(s <= 7)
        def _():
            line = gains.at[on_left]
            remote(line, line, zg_right, zg_recv.at[on_left], z_next, d).start()

        @pl.when((s >= 1) & (s <= 7))
        def _():
            await_recv(gains.at[on_right], zg_recv.at[on_right])

        @pl.when(s <= 6)
        def _():
            line = gains.at[on_right]
            remote(line, line, zg_left, zg_recv.at[on_right], z_before, d).start()

    line_step(0, 0)
    gain_step(0)
    loop(1, GROUPS, send_half)
    for copy in owned[2:]:
        copy.wait()

    def send_rows(k):
        to = (z + k) % SECTIONS
        remote(rows_out.at[to], rows_in.at[z], rows_send, rows_recv, to, d).start()

    def place_halves():
        await_recv(half_in.at[pl.ds(0, GROUPS - 1)], half_recv)
        arrived = half_in[...]
        slot = jnp.broadcast_to(arrived[:, 4:5, HEAD // 2:HEAD // 2 + 1], (GROUPS, ROWS, 1))
        slot = slot.reshape(2 * TILE, 1)
        arrived = arrived.reshape(2 * TILE, HEAD).astype(BF16)
        row = lax.broadcasted_iota(jnp.int32, (2 * TILE, TILE), 0) % ROWS
        col = lax.broadcasted_iota(jnp.int32, (2 * TILE, TILE), 1)
        same = slot == (col // (ROWS // 2)).astype(F32)
        place = jnp.where(same & (row == col % (ROWS // 2)), 1.0, 0.0).astype(BF16)
        place_tags = jnp.where(same & (row == col % (ROWS // 2) + ROWS // 2), 1.0, 0.0).astype(BF16)
        placing[...] = place
        rows_out[...] = dot(place, arrived, 0, 0).reshape(SECTIONS, ROWS, HEAD)
        home_out[pl.ds(0, SECTIONS)] = dot(place_tags, arrived, 0, 0).reshape(SECTIONS, ROWS, HEAD)
        rows_in[z] = rows_out[z]

        loop(1, SECTIONS, send_rows)

        tags = home_out[z]
        document = jnp.broadcast_to(tags[:, 0:1], (ROWS, TILE))
        position = jnp.broadcast_to(tags[:, HEAD // 4:HEAD // 4 + 1], (ROWS, TILE))
        lane = lax.broadcasted_iota(jnp.int32, (ROWS, TILE), 1) % ROWS
        mine = lane == lax.broadcasted_iota(jnp.int32, (ROWS, TILE), 0)
        query_document = jnp.sum(jnp.where(mine, document, 0.0), axis=0, keepdims=True)
        query_position = jnp.sum(jnp.where(mine, position, 0.0), axis=0, keepdims=True)
        allowed = (document == query_document) & (position <= query_position)
        bias[...] = jnp.where(allowed, 0.0, NEGATIVE)
        lane = lax.broadcasted_iota(jnp.int32, (ROWS, HEAD), 1)
        power = (lane % (HEAD // 2)).astype(F32) * (-2.0 / HEAD)
        angles = position * jnp.exp(power * math.log(ROPE_BASE))
        sine = jnp.sin(angles)
        turns[0] = jnp.cos(angles)
        turns[1] = jnp.where(lane < HEAD // 2, -sine, sine)

    def take_rows():
        await_recv(rows_in.at[pl.ds(0, SECTIONS - 1)], rows_recv)
        current[...] = rows_in[...].reshape(TILE, HEAD)

    def partner(j):
        return (z + jnp.where(j % 2 == 1, (j + 1) // 2, SECTIONS - j // 2)) % SECTIONS

    def send_packed(v, j):
        to = partner(j)
        remote(packed_all.at[v * SECTIONS + to], packed_in.at[v, z],
               packed_send.at[v], packed_recv.at[v], to, d).start()

    def send_pairs(v, j):
        to = partner(j)
        remote(pairs_all.at[v * SECTIONS + to], pairs_in.at[v, z],
               pair_send.at[v], pair_recv.at[v], to, d).start()

    def forward(layer):
        cosine, sine = turns[0], turns[1]
        cosine_all, sine_all = over_heads(cosine), over_heads(sine)
        x = current[...]
        saved[layer] = x
        gained = x * gain_rows(gains[layer % SECTIONS, layer // SECTIONS])
        pre = dot(side_by_side(gained).astype(BF16),
                  weight[layer].reshape(FEATURES, 2 * HEAD), 1, 0)
        scale = lax.rsqrt(row_mean(x * x) + EPSILON)
        saved_scale[layer] = scale
        pre = pre * scale
        normed = gained * over_heads(scale)
        queries = turn(normed, cosine_all, sine_all).astype(BF16)
        keys = turn(pre[:, :HEAD], cosine, sine).astype(BF16)
        values = pre[:, HEAD:].astype(BF16)
        scores = dot(keys, queries, 1, 1) * HEAD ** (-0.5) + bias[...]
        raised = jnp.exp(scores - jnp.max(scores, axis=0, keepdims=True))
        weights = raised / jnp.sum(raised, axis=0, keepdims=True)
        saved_queries[layer] = queries
        saved_keys[layer, 0] = keys
        saved_keys[layer, 1] = values
        saved_weights[layer] = weights
        wide = side_by_side(normed)
        packed_all[layer] = jnp.concatenate(
            [wide[:, :FEATURES // 2], wide[:, FEATURES // 2:]], axis=0).astype(BF16)
        current[...] = x + dot(weights.astype(BF16), values, 0, 0)

    def rows_at(layer, e, at, rows):
        if e == 0:
            return weight.at[layer, :, at, core, rows, :]
        return weight.at[layer, at, :, core, rows, :]

    def device_by(e, by):
        if e == 0:
            return (px * SIDE + (py + by) % SIDE) * 2 + core
        return (((px + by) % SIDE) * SIDE + py) * 2 + core

    def around(e, by):
        return ((py if e == 0 else px) + by) % SIDE

    every, low, high = pl.ds(0, PART), pl.ds(0, PART // 2), pl.ds(PART // 2, PART // 2)

    def stage_one(layer, e):
        line = rows_at(layer, e, around(e, 0), every)
        remote(line, line, ring_send.at[layer // SECTIONS, 0], ring_recv.at[layer, 0], z, device_by(e, 1)).start()
        remote(line, line, ring_send.at[layer // SECTIONS, 0], ring_recv.at[layer, 1], z, device_by(e, 3)).start()

    def stage_two(layer, e):
        left, right = around(e, 3), around(e, 1)
        await_recv(rows_at(layer, e, left, every), ring_recv.at[layer, 0])
        part = rows_at(layer, e, left, low)
        remote(part, part, ring_send.at[layer // SECTIONS, 1], ring_recv.at[layer, 2], z, device_by(e, 1)).start()
        await_recv(rows_at(layer, e, right, every), ring_recv.at[layer, 1])
        part = rows_at(layer, e, right, high)
        remote(part, part, ring_send.at[layer // SECTIONS, 1], ring_recv.at[layer, 3], z, device_by(e, 3)).start()

    def stage_three(layer, e):
        far = around(e, 2)
        await_recv(rows_at(layer, e, far, low), ring_recv.at[layer, 2])
        await_recv(rows_at(layer, e, far, high), ring_recv.at[layer, 3])
        half = weight.at[layer, :, :, core]
        remote(half, half, ring_send.at[layer // SECTIONS, 2], ring_recv.at[layer, 4], z, twin).start()

    def stage_four(layer, e):
        await_recv(weight.at[layer, :, :, 1 - core], ring_recv.at[layer, 4])

    def turn_of(t):
        @pl.when((t >= 1) & (t <= 8))
        def _():
            line_step(0, t)
            gain_step(t)

        @pl.when((t <= 7) & (t % 2 == 1))
        def _():
            line_step(1, t // 2)

        @pl.when((t >= 8) & (t <= 12))
        def _():
            line_step(1, t - 4)

        for late, stage in ((0, stage_one), (1, stage_two), (2, stage_three), (3, stage_four)):
            v = jnp.where(t - late <= 8, 0, 1)
            s = t - late - 8 * v

            @pl.when((s >= 1) & (s <= 8))
            def _():
                stage(v * SECTIONS + (z + SECTIONS - s) % SECTIONS, 0)

            @pl.when((s >= 1) & (s <= 7))
            def _():
                stage(v * SECTIONS + (z + s) % SECTIONS, 1)

        @pl.when(t == 9)
        def _():
            place_halves()

        @pl.when(t == 11)
        def _():
            take_rows()

        @pl.when((t >= 11) & (t <= 14))
        def _():
            loop(4 * (t - 11), 4 * (t - 11) + 4, forward)

        @pl.when(t == 14)
        def _():
            loop(1, SECTIONS, lambda j: send_packed(0, j))

    loop(1, 20, turn_of)

    loop(SECTIONS, LAYERS, forward)

    last_copy.wait()
    both = last[...].astype(F32)
    current[...] = stacked(jnp.where(z % 2 == 0, both[:ROWS], both[ROWS:]))

    def backward(step):
        layer = LAYERS - 1 - step
        cosine, sine = turns[0], turns[1]
        cosine_all, sine_all = over_heads(cosine), over_heads(sine)
        upstream = current[...]
        rounded = upstream.astype(BF16)
        keys = saved_keys[layer, 0]
        values = saved_keys[layer, 1]
        queries = saved_queries[layer]
        weights = saved_weights[layer]
        d_weights = dot(values, rounded, 1, 1)
        d_values = dot(weights.astype(BF16), rounded, 1, 0)
        inner = jnp.sum(d_weights * weights, axis=0, keepdims=True)
        d_scores = ((weights * HEAD ** (-0.5)) * (d_weights - inner)).astype(BF16)
        d_keys = dot(d_scores, queries, 1, 0)
        d_key_pre = unturn(d_keys, cosine, sine)
        pair = jnp.concatenate([d_key_pre, d_values], axis=1).astype(BF16)
        d_packed = stacked(dot(pair, weight[layer].reshape(FEATURES, 2 * HEAD), 1, 1))
        pairs_all[layer] = jnp.concatenate([d_key_pre, d_values], axis=0).astype(BF16)
        d_queries = dot(d_scores, keys, 0, 0)
        inside = jnp.sum((d_queries * queries.astype(F32)).reshape(HEADS, ROWS, HEAD), axis=0)
        inside = inside + d_keys * keys.astype(F32) + d_values * values.astype(F32)
        scale = saved_scale[layer]
        pull = jnp.sum(inside, axis=-1, keepdims=True) * (scale * scale * (1.0 / FEATURES))
        by = gain_rows(gains[layer % SECTIONS, layer // SECTIONS]) * over_heads(scale)
        known = upstream - saved[layer] * over_heads(pull)
        known = known + unturn(d_queries, cosine_all, sine_all) * by
        current[...] = known + d_packed * by

    def terms_of(v):
        others = pl.ds(0, SECTIONS - 1)
        await_recv(packed_in.at[v, others], packed_recv.at[v])
        await_recv(pairs_in.at[v, others], pair_recv.at[v])
        packed_in[v, z] = packed_all[v * SECTIONS + z]
        pairs_in[v, z] = pairs_all[v * SECTIONS + z]
        pair = pairs_in[v].astype(F32)
        pair = jnp.concatenate([pair[:, :ROWS], pair[:, ROWS:]], axis=2)
        nothing = jnp.zeros_like(pair)
        upper = jnp.concatenate([pair, nothing], axis=1).reshape(2 * TILE, 2 * HEAD)
        lower = jnp.concatenate([nothing, pair], axis=1).reshape(2 * TILE, 2 * HEAD)
        both = jnp.concatenate([upper, lower], axis=1).astype(BF16)
        product = dot(packed_in[v].reshape(2 * TILE, FEATURES // 2), both, 0, 0).astype(BF16)
        for g in range(GROUPS):
            rows = product[PART * (g % 16):PART * (g % 16 + 1)]
            terms[v, g // 2, g % 2] = rows[:, 2 * HEAD * (g // 16):2 * HEAD * (g // 16 + 1)]
        remote(terms.at[v, :, 1 - core], twin_in.at[v],
               twin_send.at[v], twin_recv.at[v], z, twin).start()

    def send_chips(v):
        await_recv(twin_in.at[v], twin_recv.at[v])
        chip_terms[v] = (terms[v, :, core].astype(F32) + twin_in[v].astype(F32)).astype(BF16)

        def send_chip(k):
            to = (chip + k) % (GROUPS // 2)
            remote(chip_terms.at[v, to], chip_in.at[v, chip],
                   chip_send.at[v], chip_recv.at[v], z, 2 * to + core).start()

        loop(1, GROUPS // 2, send_chip)
        chip_in[v, chip] = chip_terms[v, chip]

    def backward_step(j):
        backward(j)

        @pl.when((j >= 1) & (j < 8))
        def _():
            send_packed(1, 2 * j - 1)
            send_packed(1, 2 * j)

        @pl.when(j == 8)
        def _():
            send_packed(1, SECTIONS - 1)

        @pl.when((j >= SECTIONS) & (j < SECTIONS + 8))
        def _():
            send_pairs(1, 2 * (j - SECTIONS) + 1)

        @pl.when((j >= SECTIONS) & (j < SECTIONS + 7))
        def _():
            send_pairs(1, 2 * (j - SECTIONS) + 2)

        layer = LAYERS - 1 - j

        @pl.when((j >= SECTIONS) & (layer != z))
        def _():
            remote(pairs_all.at[layer], pairs_in.at[0, z],
                   pair_send.at[0], pair_recv.at[0], layer, d).start()

    loop(0, LAYERS, backward_step)

    back_out[...] = current[...].astype(BF16).astype(F32).reshape(SECTIONS, ROWS, HEAD)
    back_in[z] = back_out[z]

    def send_back(k):
        to = (z + k) % SECTIONS
        remote(back_out.at[to], back_in.at[z], back_send, back_recv, to, d).start()

    loop(1, SECTIONS, send_back)
    terms_of(1)
    terms_of(0)
    send_chips(1)

    await_recv(back_in.at[pl.ds(0, SECTIONS - 1)], back_recv)
    mine = back_in[...].reshape(TILE, HEAD).astype(BF16)
    home_out[...] = dot(placing[...], mine, 1, 0).reshape(GROUPS, ROWS, HEAD)
    home_in[d] = home_out[d]

    def send_home(k):
        to = (d + k) % GROUPS
        remote(home_out.at[to], home_in.at[d], home_send, home_recv, z, to).start()

    loop(1, GROUPS, send_home)
    send_chips(0)

    await_recv(home_in.at[pl.ds(0, GROUPS - 1)], home_recv)
    arrived = home_in[...].reshape(2 * TILE, HEAD).astype(BF16)
    grad_ref[...] = dot(sorting[...], arrived, 0, 0).astype(BF16)

    others = pl.ds(0, SECTIONS - 1)
    for v in range(2):
        await_send(weight.at[others, pl.ds(0, 2), :, 0], ring_send.at[v, 0])
        await_send(weight.at[others, 0, :, 0], ring_send.at[v, 1])
        await_send(weight.at[others, :, :, 0], ring_send.at[v, 2])
        await_send(weight.at[pl.ds(0, 8), 0, :, 0], zw_right.at[v])
        await_send(weight.at[pl.ds(0, 7), 0, :, 0], zw_left.at[v])
        await_send(packed_all.at[others], packed_send.at[v])
        await_send(pairs_all.at[others], pair_send.at[v])
    await_send(gains.at[pl.ds(0, 8)], zg_right)
    await_send(gains.at[pl.ds(0, 7)], zg_left)
    await_send(rows_out.at[others], rows_send)
    await_send(back_out.at[others], back_send)
    await_send(half_out.at[pl.ds(0, GROUPS - 1)], half_send)
    await_send(home_out.at[pl.ds(0, GROUPS - 1)], home_send)
    for v in range(2):
        await_send(twin_in.at[v], twin_send.at[v])

        await_recv(chip_in.at[v, others], chip_recv.at[v])
        await_send(chip_terms.at[v, others], chip_send.at[v])
        total = jnp.zeros((PART, 2 * HEAD), F32)
        for k in range(GROUPS // 2):
            total = total + chip_in[v, k].astype(F32)
        key_out_ref[v] = total[:, :HEAD]
        value_out_ref[v] = total[:, HEAD:]


def run_whole(hidden, lengths, route, gain, key_weight, value_weight, cotangent):
    whole = pl.BlockSpec(memory_space=pltpu.VMEM)
    remote = pl.BlockSpec(memory_space=pl.ANY)
    dma = pltpu.SemaphoreType.DMA
    small = pltpu.VMEM((SECTIONS, ROWS, HEAD), F32)
    large = pltpu.VMEM((GROUPS, ROWS, HEAD), F32)
    chips = GROUPS // 2
    return pl.pallas_call(
        whole_kernel,
        out_shape=(
            jax.ShapeDtypeStruct((TILE, HEAD), BF16),
            jax.ShapeDtypeStruct((2, PART, HEAD), F32),
            jax.ShapeDtypeStruct((2, PART, HEAD), F32),
        ),
        in_specs=[whole] * 4 + [remote] * 3,
        out_specs=(whole, whole, whole),
        scratch_shapes=[
            pltpu.VMEM((LAYERS, SIDE, SIDE, 2, PART, 2 * HEAD), BF16),
            pltpu.VMEM((SECTIONS, 2, HEADS, HEAD), F32),
            pltpu.VMEM((TILE, HEAD), F32),
            pltpu.VMEM((LAYERS, TILE, HEAD), F32),
            pltpu.VMEM((LAYERS, TILE, HEAD), BF16),
            pltpu.VMEM((LAYERS, 2, ROWS, HEAD), BF16),
            pltpu.VMEM((LAYERS, ROWS, TILE), F32),
            pltpu.VMEM((LAYERS, ROWS, 1), F32),
            pltpu.VMEM((ROWS, TILE), F32),
            pltpu.VMEM((2, ROWS, HEAD), F32),
            pltpu.VMEM((LAYERS, 2 * ROWS, FEATURES // 2), BF16),
            pltpu.VMEM((2, SECTIONS, 2 * ROWS, FEATURES // 2), BF16),
            pltpu.VMEM((LAYERS, 2 * ROWS, HEAD), BF16),
            pltpu.VMEM((2, SECTIONS, 2 * ROWS, HEAD), BF16),
            pltpu.VMEM((2, chips, 2, PART, 2 * HEAD), BF16),
            pltpu.VMEM((2, chips, PART, 2 * HEAD), BF16),
            pltpu.VMEM((2, chips, PART, 2 * HEAD), BF16),
            pltpu.VMEM((2, chips, PART, 2 * HEAD), BF16),
            pltpu.VMEM((2 * TILE, TILE), BF16),
            pltpu.VMEM((2 * TILE, TILE), BF16),
            large, large, small, small, small, small, large, large,
            pltpu.VMEM((2 * ROWS, FEATURES), BF16),
            dma(()), dma((2, 2)),
            dma((2, SECTIONS, 2)), dma((2,)), dma((2,)),
            dma((SECTIONS,)), dma(()), dma(()),
            dma((2, 3)), dma((LAYERS, 5)),
            dma((2,)), dma((2,)), dma((2,)), dma((2,)),
            dma(()), dma(()), dma(()), dma(()),
            dma(()), dma(()), dma(()), dma(()),
            dma((2,)), dma((2,)), dma((2,)), dma((2,)),
        ],
        compiler_params=pltpu.CompilerParams(
            collective_id=0, has_side_effects=True, vmem_limit_bytes=56 * 2**20),
    )(hidden, lengths, route, gain, key_weight, value_weight, cotangent)


def body(hidden, lengths, route, gain, key_weight, value_weight, cotangent):
    shares = (2, SIDE, SIDE, 2, PART, HEAD)
    return run_whole(
        hidden, lengths.T, route.T, gain,
        key_weight.reshape(shares), value_weight.reshape(shares), cotangent)


def solution(mesh):
    placed = (
        P("dp", "pipe"),
        P("dp", None),
        P("dp", None),
        P("pipe", None),
        P("pipe", None, None),
        P("pipe", None, None),
        P("dp", None),
    )
    return jax.shard_map(
        body,
        mesh=mesh,
        in_specs=placed,
        out_specs=(P("dp", "pipe"), P("pipe", "dp", None), P("pipe", "dp", None)),
        check_vma=False,
    )
```
